32 devices in a mesh: dap: 8 (over z, x), head: 4 (over y, core).
Axes of the slice: x: 2, y: 2, z: 4, core: 2. Of those that a mesh axis runs over, the one named last changes fastest.
Arguments:
- pair: bfloat16 [128, 128, 128], P('dap'), may hold values from -600 to 600
- residue_mask: int32 [128], replicated, may hold values 0 or 1
- chain_breaks: int32 [128], replicated, may hold values 0 or 1
- w_query: bfloat16 [128, 128], P(None, 'head'), may hold values from -0.5 to 0.5
- w_key: bfloat16 [128, 128], P(None, 'head'), may hold values from -0.5 to 0.5
- w_value: bfloat16 [128, 128], P(None, 'head'), may hold values from -0.5 to 0.5
- w_gate: bfloat16 [128, 128], P(None, 'head'), may hold values from -0.5 to 0.5
- w_bias: bfloat16 [128, 4], P(None, 'head'), may hold values from -29 to 29
- w_out: bfloat16 [128, 128], P('head'), may hold values from -0.5 to 0.5
Outputs:
- update: bfloat16 [128, 128, 128], P('dap', None, 'head')
The draws below stay inside these ranges and needn't reach their ends.
All inputs are finite; a program needn't handle non-finite values.
Results may differ from the reference program's by a relative error of at most 0.019.
Values may be sent and summed in bfloat16 or wider, within the bound.
A program may use at most 64 MiB of HBM per device.

```python
import math
import jax
import jax.numpy as jnp
from jax import lax

PAIR = 128
HEADS = 4
HEAD_DIM = 32
RESIDUES = 128


def draw_pair(key, part):
    key = jax.random.fold_in(key, 11)
    first, second, third = jax.random.split(key, 3)
    entry_scale = jnp.exp(jax.random.uniform(second, (RESIDUES, RESIDUES, 1), minval=0.0, maxval=math.log(10.0)))
    channel_scale = jnp.exp(jax.random.uniform(third, (1, 1, PAIR), minval=0.0, maxval=math.log(10.0)))
    base = jnp.clip(jax.random.normal(first, (RESIDUES, RESIDUES, PAIR)), -6.0, 6.0)
    return (base * entry_scale * channel_scale).astype(jnp.bfloat16)


def draw_w_bias(key, part):
    key = jax.random.fold_in(key, 5)
    first, second = jax.random.split(key)
    base = jnp.clip(jax.random.normal(first, (PAIR, HEADS)), -4.0, 4.0)
    strength = jnp.exp(jax.random.uniform(second, (1, HEADS), minval=0.0, maxval=math.log(3.0)))
    return (base * strength * 0.0884).astype(jnp.bfloat16)


def set_ends(values, stream_key, low, high):
    place = [jax.random.randint(jax.random.fold_in(stream_key, axis), (), 0, length) for axis, length in enumerate(values.shape)]
    main_axis = values.shape.index(max(values.shape))
    next_to = place[:main_axis] + [(place[main_axis] + 1) % values.shape[main_axis]] + place[main_axis + 1:]
    return values.at[tuple(place)].set(low).at[tuple(next_to)].set(high)


def steps_of(key, dims, cuts, smallest, high):
    loudness, own = 1.0, jax.random.fold_in(key, 6)
    for dim, parts in cuts:
        heights = jnp.exp(jax.random.uniform(jax.random.fold_in(own, dim), (parts,), jnp.float32, smallest / len(cuts), high / len(cuts)))
        loudness = loudness * jnp.repeat(heights, dims[dim] // parts).reshape([-1 if axis == dim else 1 for axis in range(len(dims))])
    return loudness


def centred(stream_key, dims, width, limit, cuts=(), held_as=jnp.bfloat16):
    level = steps_of(stream_key, dims, cuts, -0.22, 0.18) if cuts else 1.0
    drawn = jax.random.normal(stream_key, dims, jnp.float32) * width * level
    return jnp.minimum(jnp.maximum(drawn, -limit), limit).astype(held_as)


def setup_inputs(seed: int = 0) -> dict:
    seeds = jax.random.split(jax.random.key(seed), 10)
    return {
        "pair": draw_pair(jax.random.fold_in(seeds[9], 71), 0),
        "residue_mask": set_ends((jax.random.randint(seeds[1], (RESIDUES,), 0, 8) < 7).astype(jnp.int32), jax.random.fold_in(seeds[1], 1), 0, 1),
        "chain_breaks": set_ends((jax.random.randint(seeds[2], (RESIDUES,), 0, 32) < 1).astype(jnp.int32), jax.random.fold_in(seeds[2], 1), 0, 1),
        "w_query": centred(seeds[3], (PAIR, HEADS * HEAD_DIM), PAIR ** -0.5, 0.5, ((1, 4),)),
        "w_key": centred(seeds[4], (PAIR, HEADS * HEAD_DIM), PAIR ** -0.5, 0.5, ((1, 4),)),
        "w_value": centred(seeds[5], (PAIR, HEADS * HEAD_DIM), PAIR ** -0.5, 0.5, ((1, 4),)),
        "w_gate": centred(seeds[6], (PAIR, HEADS * HEAD_DIM), PAIR ** -0.5, 0.5, ((1, 4),)),
        "w_bias": draw_w_bias(jax.random.fold_in(seeds[9], 71), 0),
        "w_out": centred(seeds[8], (HEADS * HEAD_DIM, PAIR), (HEADS * HEAD_DIM) ** -0.5, 0.5, ((0, 4),)),
    }


chain_penalty = 2.0
masked_score = -1000000000.0

def normalize(pair):
    x = pair.astype(jnp.float32)
    mean = lax.optimization_barrier(jnp.mean(x, -1, keepdims=True))
    centered = x - mean
    variance = lax.optimization_barrier(jnp.mean(centered * centered, -1, keepdims=True))
    return (centered * lax.rsqrt(variance + 1e-05)).astype(jnp.bfloat16)

def reference(pair, residue_mask, chain_breaks, w_query, w_key, w_value, w_gate, w_bias, w_out):
    normed = normalize(pair)
    query = (jnp.dot(normed, w_query, preferred_element_type=jnp.float32) * HEAD_DIM ** (-0.5)).astype(jnp.bfloat16)
    keys = jnp.dot(normed, w_key, preferred_element_type=jnp.float32).astype(jnp.bfloat16)
    values = jnp.dot(normed, w_value, preferred_element_type=jnp.float32).astype(jnp.bfloat16)
    gate = jax.nn.sigmoid(jnp.dot(normed, w_gate, preferred_element_type=jnp.float32)).astype(jnp.bfloat16)
    bias = jnp.dot(normed, w_bias, preferred_element_type=jnp.float32).astype(jnp.bfloat16)
    bias = jnp.transpose(bias, (2, 0, 1)).astype(jnp.float32)
    chain = jnp.cumsum(chain_breaks).astype(jnp.int32)
    penalty = jnp.where(chain[:, None] == chain[None, :], 0.0, -chain_penalty).astype(jnp.float32)
    keep = residue_mask[:, None] > 0

    def column(index):
        q = lax.dynamic_index_in_dim(query, index, 1, keepdims=False).reshape(RESIDUES, HEADS, HEAD_DIM).astype(jnp.float32)
        k = lax.dynamic_index_in_dim(keys, index, 1, keepdims=False).reshape(RESIDUES, HEADS, HEAD_DIM).astype(jnp.float32)
        v = lax.dynamic_index_in_dim(values, index, 1, keepdims=False).reshape(RESIDUES, HEADS, HEAD_DIM).astype(jnp.float32)
        scores = jnp.einsum('khc,ihc->hki', k, q) + bias + penalty
        scores = jnp.where(keep, scores, masked_score)
        weights = jax.nn.softmax(scores, axis=1).astype(jnp.bfloat16).astype(jnp.float32)
        result = jnp.einsum('hki,khc->ihc', weights, v)
        return result.astype(jnp.bfloat16).reshape(RESIDUES, HEADS * HEAD_DIM)
    attended = lax.map(column, jnp.arange(RESIDUES, dtype=jnp.int32))
    attended = jnp.swapaxes(attended, 0, 1)
    gated = (gate.astype(jnp.float32) * attended.astype(jnp.float32)).astype(jnp.bfloat16)
    return jnp.dot(gated, w_out, preferred_element_type=jnp.float32).astype(jnp.bfloat16)
```

```python
import functools

import jax
import jax.numpy as jnp
from jax import lax
from jax.experimental import pallas as pl
from jax.experimental.pallas import tpu as pltpu
from jax.sharding import PartitionSpec as P

chain_penalty = 2.0
masked_score = -1000000000.0
LANES = 128
MESH = pl.DeviceIdType.MESH
f32 = jnp.float32
bf16 = jnp.bfloat16


def nn(a, b):
    return lax.dot_general(a, b, (((1,), (0,)), ((), ())), preferred_element_type=f32)


def nt(a, b):
    return lax.dot_general(a, b, (((1,), (1,)), ((), ())), preferred_element_type=f32)


def tn(a, b):
    return lax.dot_general(a, b, (((0,), (0,)), ((), ())), preferred_element_type=f32)


def each(count, do, start=0, most=8):
    if count - start <= most:
        for index in range(start, count):
            do(index)
    else:
        pl.loop(start, count)(do)


def lanes_at(place):
    return pl.ds(pl.multiple_of(place * LANES, LANES), LANES)


def ones_where(condition):
    return jnp.where(condition, 1.0, 0.0).astype(bf16)


def iota(shape, axis):
    return lax.broadcasted_iota(jnp.int32, shape, axis)


def normalize(x, average):
    mean = nn(x, average)
    centered = x.astype(f32) - mean
    square = centered * centered
    high = square.astype(bf16)
    low = (square - high.astype(f32)).astype(bf16)
    variance = nn(high, average) + nn(low, average)
    return (centered * lax.rsqrt(variance + 1e-05)).astype(bf16)


def kernel(
    groups, heads,
    pair, mask, breaks, wq, wk, wv, wg, wb, wo,
    out,
    stage, x, weights, bias, wide, chain_column, chain_row, keep,
    query, keys, values_t, gate_t, gated, result, landed, leave, arrive,
    x_send, x_recv, w_send, w_recv, b_send, b_recv, r_send, r_recv,
):
    rows, total, channels = pair.shape
    width = wq.shape[0]
    devices = groups * heads
    block = total // groups
    columns = total // devices
    d = lax.axis_index("dap")
    h = lax.axis_index("head")
    me = d * heads + h
    my_rows = pl.ds(pl.multiple_of(d * rows, rows), rows)

    def peer(offset):
        other = lax.rem(me + offset, devices)
        return other, other // heads, lax.rem(other, heads)

    barrier = pltpu.get_barrier_semaphore()

    @pl.loop(1, devices)
    def _(offset):
        _, pd, ph = peer(offset)
        pl.semaphore_signal(barrier, inc=1, device_id=(pd, ph), device_id_type=MESH)

    taken = columns * rows
    out_row = iota((taken, rows * block), 0)
    in_row = iota((taken, rows * block), 1)
    select = ones_where(
        in_row == lax.rem(out_row, rows) * block + h * columns + out_row // rows
    )

    def selected(group):
        part = pair[:, pl.ds(pl.multiple_of(group * block, block), block), :]
        return nn(select, part.reshape(rows * block, channels)).astype(bf16)

    def fill(offset):
        part = selected(lax.rem(d + offset, groups))
        stage[offset] = part.reshape(columns, rows, channels)

    each(groups, fill, start=1)
    x[:, my_rows, :] = selected(d).reshape(columns, rows, channels)

    for place, matrix in enumerate((wq, wk, wv, wg, wo)):
        weights[h, place * width : (place + 1) * width, :] = matrix[...]

    pl.semaphore_wait(barrier, devices - 1)

    def x_copy(offset, slot, target):
        return pltpu.make_async_remote_copy(
            src_ref=stage.at[offset],
            dst_ref=x.at[:, pl.ds(pl.multiple_of(slot * rows, rows), rows), :],
            send_sem=x_send.at[offset],
            recv_sem=x_recv.at[slot],
            device_id=(target, h),
            device_id_type=MESH,
        )

    def w_copy(offset, slot, target):
        return pltpu.make_async_remote_copy(
            src_ref=weights.at[slot],
            dst_ref=weights.at[slot],
            send_sem=w_send.at[offset],
            recv_sem=w_recv.at[slot],
            device_id=(d, target),
            device_id_type=MESH,
        )

    def b_copy(offset, source_d, source_h, pd, ph):
        place = pl.ds(pl.multiple_of(source_d * rows, rows), rows)
        return pltpu.make_async_remote_copy(
            src_ref=bias.at[source_h, place, :],
            dst_ref=bias.at[source_h, place, :],
            send_sem=b_send.at[offset],
            recv_sem=b_recv.at[source_d * heads + source_h],
            device_id=(pd, ph),
            device_id_type=MESH,
        )

    def r_copy(offset, slot, other, pd, ph):
        return pltpu.make_async_remote_copy(
            src_ref=result.at[other],
            dst_ref=landed.at[slot],
            send_sem=r_send.at[offset],
            recv_sem=r_recv.at[slot],
            device_id=(pd, ph),
            device_id_type=MESH,
        )

    @pl.loop(1, groups)
    def _(offset):
        x_copy(offset, d, lax.rem(d + offset, groups)).start()

    @pl.loop(1, heads)
    def _(offset):
        w_copy(offset, h, lax.rem(h + offset, heads)).start()

    average = jnp.full((channels, channels), 1.0 / channels, f32).astype(bf16)
    wb_rows = jnp.broadcast_to(wb[...].astype(f32), (rows, channels)).astype(bf16)
    bias_row = iota((rows, LANES), 0)

    def bias_block(place):
        span = lanes_at(place)
        entries = pair[:, span, :].reshape(rows * LANES, channels)
        normed = normalize(entries, average)
        found = jnp.zeros((rows, LANES), f32)
        for row in range(rows):
            line = nt(wb_rows, normed[row * LANES : (row + 1) * LANES])
            found = jnp.where(bias_row == row, line, found)
        bias[h, my_rows, span] = found.astype(bf16)

    each(total // LANES, bias_block, most=1)

    @pl.loop(1, devices)
    def _(offset):
        _, pd, ph = peer(offset)
        b_copy(offset, d, h, pd, ph).start()

    tall = iota((total, total), 0)
    across = iota((total, total), 1)
    breaks_row = jnp.broadcast_to(breaks[...].astype(f32), (LANES, total)).astype(bf16)
    mask_row = jnp.broadcast_to(mask[...].astype(f32), (LANES, total)).astype(bf16)
    chain_column[...] = nt(ones_where(across <= tall), breaks_row)
    keep[...] = nt(ones_where(across == tall), mask_row)
    chain_row[...] = nn(breaks_row[:8], ones_where(tall <= across))

    out_lanes = heads * columns * width
    channel = iota((channels, out_lanes), 0)
    lane = iota((channels, out_lanes), 1)
    share = lane // (columns * width)
    column_of_lane = lax.rem(lane, columns * width) // width
    source = share * width + lax.rem(lane, width)

    ordered = columns * LANES
    first = iota((ordered, ordered), 0)
    second = iota((ordered, ordered), 1)
    inner = lax.rem(first, LANES)
    leave[...] = ones_where(
        second
        == lax.rem(inner, columns) * LANES + inner // columns * columns + first // LANES
    )
    inner = lax.rem(second, LANES)
    arrive[...] = ones_where(
        first
        == inner // columns * rows + second // LANES * columns + lax.rem(inner, columns)
    )

    @pl.loop(1, heads)
    def _(offset):
        other = lax.rem(h + offset, heads)
        w_copy(offset, other, other).wait_recv()

    wo_full = jnp.concatenate([weights[k, 4 * width : 5 * width, :] for k in range(heads)], axis=0)
    for column in range(columns):
        placed = ones_where((channel == source) & (column_of_lane == column))
        wide[column * channels : (column + 1) * channels, :] = nn(wo_full, placed).astype(bf16)
    wq_t, wk_t, wv_t, wg_t = (
        jnp.concatenate(
            [weights[k, place * width : (place + 1) * width, :] for k in range(heads)], axis=0
        )
        for place in range(4)
    )

    @pl.loop(1, groups)
    def _(offset):
        other = lax.rem(d + offset, groups)
        x_copy(offset, other, other).wait_recv()

    for column in range(columns):
        normed = normalize(x[column], average)
        query[column] = (nt(normed, wq_t) * width ** (-0.5)).astype(bf16)
        keys[column] = nt(normed, wk_t).astype(bf16)
        values_t[column] = nt(wv_t, normed).astype(bf16)
        gate_t[column] = jax.nn.sigmoid(nt(wg_t, normed)).astype(bf16)

    @pl.loop(1, devices)
    def _(offset):
        other, pd, ph = peer(offset)
        b_copy(offset, pd, ph, pd, ph).wait_recv()

    head_of_lane = iota((total, heads * width), 1) // width

    def attend(place):
        span = lanes_at(place)
        penalty = jnp.where(chain_column[...] == chain_row[:1, span], 0.0, -chain_penalty)
        for head in range(heads):
            added = bias[head, :, span].astype(f32) + penalty
            share_t = slice(head * width, (head + 1) * width)

            def attend_column(column):
                own = keys[column]
                own = jnp.where(head_of_lane == head, own, jnp.zeros_like(own))
                scores = nt(own, query[column, span, :]) + added
                scores = jnp.where(keep[...] > 0.5, scores, masked_score)
                expo = jnp.exp(scores - jnp.max(scores, axis=0, keepdims=True))
                scale = 1.0 / jnp.sum(expo, axis=0, keepdims=True)
                attended = nn(values_t[column, share_t, :], (expo * scale).astype(bf16))
                gated[column, share_t, span] = (
                    gate_t[column, share_t, span].astype(f32) * attended.astype(bf16).astype(f32)
                ).astype(bf16)

            each(columns, attend_column, most=columns if total == LANES else 1)

    each(total // LANES, attend, most=1)

    packed_lanes = columns * width

    def project(place):
        span = lanes_at(place)
        mine = jnp.concatenate([gated[column, :, span] for column in range(columns)], axis=1)
        mine = nt(leave[...], mine).astype(bf16)
        mine = jnp.concatenate(
            [mine[part * LANES : (part + 1) * LANES] for part in range(columns)], axis=1
        )
        update = nn(mine, wide[...]).astype(bf16)
        for part in range(LANES // rows):
            for head in range(heads):
                result[(place * (LANES // rows) + part) * heads + head] = update[
                    part * rows : (part + 1) * rows,
                    head * packed_lanes : (head + 1) * packed_lanes,
                ]

    each(total // LANES, project, most=1)

    @pl.loop(1, devices)
    def _(offset):
        other, pd, ph = peer(offset)
        r_copy(offset, me, other, pd, ph).start()

    landed[me] = result[me]

    @pl.loop(1, devices)
    def _(offset):
        other, pd, ph = peer(offset)
        r_copy(offset, other, other, pd, ph).wait_recv()

    sources = LANES // columns

    def settle(place):
        came = landed[pl.ds(place * sources, sources)].reshape(sources * rows, packed_lanes)
        moved = tn(came, arrive[...]).astype(bf16)
        for row in range(rows):
            part, line = row // columns, row % columns
            out[row, :, lanes_at(place)] = moved[
                line * width : (line + 1) * width, part * LANES : (part + 1) * LANES
            ]

    each(total // LANES, settle, most=1)

    @pl.loop(1, groups)
    def _(offset):
        x_copy(offset, d, lax.rem(d + offset, groups)).wait_send()

    @pl.loop(1, heads)
    def _(offset):
        w_copy(offset, h, lax.rem(h + offset, heads)).wait_send()

    @pl.loop(1, devices)
    def _(offset):
        other, pd, ph = peer(offset)
        b_copy(offset, d, h, pd, ph).wait_send()
        r_copy(offset, me, other, pd, ph).wait_send()


def body(groups, heads, pair, residue_mask, chain_breaks, w_query, w_key, w_value, w_gate, w_bias, w_out):
    rows, total, channels = pair.shape
    width = w_query.shape[1]
    devices = groups * heads
    columns = total // devices
    packed_lanes = columns * width
    assert packed_lanes == LANES and columns * columns == rows
    dma = pltpu.SemaphoreType.DMA
    update = pl.pallas_call(
        functools.partial(kernel, groups, heads),
        out_shape=jax.ShapeDtypeStruct((rows, width, total), bf16),
        in_specs=[pl.BlockSpec(memory_space=pltpu.VMEM)] * 9,
        out_specs=pl.BlockSpec(memory_space=pltpu.VMEM),
        scratch_shapes=[
            pltpu.VMEM((groups, columns, rows, channels), bf16),
            pltpu.VMEM((columns, total, channels), bf16),
            pltpu.VMEM((heads, 5 * width, channels), bf16),
            pltpu.VMEM((heads, total, total), bf16),
            pltpu.VMEM((columns * channels, heads * packed_lanes), bf16),
            pltpu.VMEM((total, LANES), f32),
            pltpu.VMEM((8, total), f32),
            pltpu.VMEM((total, LANES), f32),
            pltpu.VMEM((columns, total, channels), bf16),
            pltpu.VMEM((columns, total, channels), bf16),
            pltpu.VMEM((columns, channels, total), bf16),
            pltpu.VMEM((columns, channels, total), bf16),
            pltpu.VMEM((columns, channels, total), bf16),
            pltpu.VMEM((devices, rows, packed_lanes), bf16),
            pltpu.VMEM((devices, rows, packed_lanes), bf16),
            pltpu.VMEM((columns * LANES, columns * LANES), bf16),
            pltpu.VMEM((columns * LANES, columns * LANES), bf16),
            dma((groups,)), dma((groups,)),
            dma((heads,)), dma((heads,)),
            dma((devices,)), dma((devices,)),
            dma((devices,)), dma((devices,)),
        ],
        compiler_params=pltpu.CompilerParams(
            collective_id=0, has_side_effects=True, vmem_limit_bytes=52 * 2**20
        ),
    )(
        pair, residue_mask.reshape(1, total), chain_breaks.reshape(1, total),
        w_query.T, w_key.T, w_value.T, w_gate.T, w_bias.T, w_out,
    )
    return jnp.swapaxes(update, 1, 2)


def solution(mesh):
    placed = (
        P("dap", None, None),
        P(),
        P(),
        P(None, "head"),
        P(None, "head"),
        P(None, "head"),
        P(None, "head"),
        P(None, "head"),
        P("head", None),
    )
    return jax.shard_map(
        functools.partial(body, mesh.shape["dap"], mesh.shape["head"]),
        mesh=mesh, in_specs=placed, out_specs=P("dap", None, "head"), check_vma=False,
    )
```

```python
import functools

import jax
import jax.numpy as jnp
from jax import lax
from jax.experimental import pallas as pl
from jax.experimental.pallas import tpu as pltpu
from jax.sharding import PartitionSpec as P

chain_penalty = 2.0
masked_score = -1000000000.0
LANES = 128
MESH = pl.DeviceIdType.MESH
f32 = jnp.float32
bf16 = jnp.bfloat16


def nn(a, b):
    return lax.dot_general(a, b, (((1,), (0,)), ((), ())), preferred_element_type=f32)


def nt(a, b):
    return lax.dot_general(a, b, (((1,), (1,)), ((), ())), preferred_element_type=f32)


def tn(a, b):
    return lax.dot_general(a, b, (((0,), (0,)), ((), ())), preferred_element_type=f32)


def each(count, do, start=0, most=8):
    if count - start <= most:
        for index in range(start, count):
            do(index)
    else:
        pl.loop(start, count)(do)


def lanes_at(place):
    return pl.ds(pl.multiple_of(place * LANES, LANES), LANES)


def ones_where(condition):
    return jnp.where(condition, 1.0, 0.0).astype(bf16)


def iota(shape, axis):
    return lax.broadcasted_iota(jnp.int32, shape, axis)


def normalize(x, average):
    mean = nn(x, average)
    centered = x.astype(f32) - mean
    square = centered * centered
    high = square.astype(bf16)
    low = (square - high.astype(f32)).astype(bf16)
    variance = nn(high, average) + nn(low, average)
    return (centered * lax.rsqrt(variance + 1e-05)).astype(bf16)


def kernel(
    groups, heads,
    pair_in, mask_in, breaks_in, wq, wk, wv, wg, wb_in, wo,
    out,
    pair, mask, breaks, wb, stage, x, weights, wb_all, bias, wide, chain_column, chain_row, keep,
    query, keys, values_t, gate_t, gated, result, landed, leave, arrive,
    in_sem, x_sem, w_sem, wb_sem, b_sem, r_sem,
):
    rows, total, channels = pair.shape
    width = wq.shape[0]
    devices = groups * heads
    block = total // groups
    columns = total // devices
    d = lax.axis_index("dap")
    h = lax.axis_index("head")
    me = d * heads + h
    my_rows = pl.ds(pl.multiple_of(d * rows, rows), rows)

    def around(place, offset, count):
        moved = place + offset
        return jnp.where(moved >= count, moved - count, moved)

    def others(do):
        for offset in range(1, heads):
            do(d, around(h, offset, heads))

        def at_group(offset):
            group = around(d, offset, groups)
            for head_offset in range(heads):
                do(group, around(h, head_offset, heads))

        pl.loop(1, groups)(at_group)

    loads = [
        pltpu.make_async_copy(source, target, in_sem.at[place])
        for place, (source, target) in enumerate(
            [(pair_in, pair), (wb_in, wb)]
            + [
                (matrix, weights.at[h, place * width : (place + 1) * width, :])
                for place, matrix in enumerate((wq, wk, wv, wg, wo))
            ]
            + [(mask_in, mask), (breaks_in, breaks)]
        )
    ]
    for load in loads:
        load.start()

    barrier = pltpu.get_barrier_semaphore()

    def greet(pd, ph):
        pl.semaphore_signal(barrier, inc=1, device_id=(pd, ph), device_id_type=MESH)

    others(greet)

    taken = columns * rows
    in_row = iota((1, rows * block), 1)
    column = lax.rem(in_row, block) - h * columns
    wanted = jnp.where((column >= 0) & (column < columns), column * rows + in_row // block, -1)
    select = ones_where(iota((taken, rows * block), 0) == wanted)
    loads[0].wait()

    def selected(group):
        part = pair[:, pl.ds(pl.multiple_of(group * block, block), block), :]
        return nn(select, part.reshape(rows * block, channels)).astype(bf16)

    def fill(offset):
        part = selected(around(d, offset, groups))
        stage[offset] = part.reshape(columns, rows, channels)

    each(groups, fill, start=1)
    x[:, my_rows, :] = selected(d).reshape(columns, rows, channels)

    for load in loads[1:]:
        load.wait()
    wb_all[h] = jnp.broadcast_to(wb[...].astype(f32), (rows, channels)).astype(bf16)
    pl.semaphore_wait(barrier, devices - 1)

    def send(source, target, sems, pd, ph):
        return pltpu.make_async_remote_copy(
            src_ref=source,
            dst_ref=target,
            send_sem=sems.at[0],
            recv_sem=sems.at[1],
            device_id=(pd, ph),
            device_id_type=MESH,
        )

    def all_copies(part, sems):
        return send(part, part, sems, d, around(h, 1, heads))

    all_x = all_copies(stage.at[pl.ds(0, groups - 1)], x_sem)
    all_w = all_copies(weights.at[pl.ds(0, heads - 1)], w_sem)
    all_wb = all_copies(wb_all.at[pl.ds(0, heads - 1)], wb_sem)
    all_b = all_copies(bias.at[:, pl.ds(0, (groups - 1) * rows), :], b_sem)
    all_r = all_copies(landed.at[pl.ds(0, devices - 1)], r_sem)

    for offset in range(1, heads):
        send(wb_all.at[h], wb_all.at[h], wb_sem, d, around(h, offset, heads)).start()

    @pl.loop(1, groups)
    def _(offset):
        send(stage.at[offset], x.at[:, my_rows, :], x_sem, around(d, offset, groups), h).start()

    for offset in range(1, heads):
        send(weights.at[h], weights.at[h], w_sem, d, around(h, offset, heads)).start()

    average = jnp.full((channels, channels), 1.0 / channels, f32).astype(bf16)
    bias_row = lax.rem(iota((heads * rows, LANES), 0), rows)

    def bias_block(place, arrived=True):
        span = lanes_at(place)
        entries = pair[:, span, :].reshape(rows * LANES, channels)
        normed = normalize(entries, average)
        if not arrived:
            all_wb.wait_recv()
        wb_rows = wb_all[...].reshape(heads * rows, channels)
        found = jnp.zeros((heads * rows, LANES), f32)
        for row in range(rows):
            line = nt(wb_rows, normed[row * LANES : (row + 1) * LANES])
            found = jnp.where(bias_row == row, line, found)
        bias[:, my_rows, span] = found.astype(bf16).reshape(heads, rows, LANES)

    bias_block(0, arrived=False)
    if total > LANES:
        pl.loop(1, total // LANES)(bias_block)

    @pl.loop(1, groups)
    def _(offset):
        part = bias.at[:, my_rows, :]
        send(part, part, b_sem, around(d, offset, groups), h).start()

    tall = iota((total, total), 0)
    across = iota((total, total), 1)
    breaks_row = jnp.broadcast_to(breaks[...].astype(f32), (LANES, total)).astype(bf16)
    mask_row = jnp.broadcast_to(mask[...].astype(f32), (LANES, total)).astype(bf16)
    chain_column[...] = nt(ones_where(across <= tall), breaks_row)
    keep[...] = nt(ones_where(across == tall), mask_row)
    chain_row[...] = nn(breaks_row[:8], ones_where(tall <= across))

    out_lanes = heads * columns * width
    lane = iota((1, out_lanes), 1)
    lane_column = lax.rem(lane, columns * width) // width
    lane_source = lane // (columns * width) * width + lax.rem(lane, width)
    channel = iota((channels, out_lanes), 0)

    ordered = columns * LANES
    first = iota((ordered, ordered), 0)
    second = iota((1, ordered), 1)
    entry = lax.rem(second, LANES)
    leave[...] = ones_where(
        first
        == lax.rem(entry, columns) * LANES + entry // columns * columns + second // LANES
    )
    arrive[...] = ones_where(
        first
        == entry // columns * rows + second // LANES * columns + lax.rem(entry, columns)
    )

    all_w.wait_recv()
    wo_full = jnp.concatenate([weights[k, 4 * width : 5 * width, :] for k in range(heads)], axis=0)
    for column in range(columns):
        placed = ones_where(channel == jnp.where(lane_column == column, lane_source, -1))
        wide[column * channels : (column + 1) * channels, :] = nn(wo_full, placed).astype(bf16)
    wq_t, wk_t, wv_t, wg_t = (
        jnp.concatenate(
            [weights[k, place * width : (place + 1) * width, :] for k in range(heads)], axis=0
        )
        for place in range(4)
    )

    all_x.wait_recv()
    for column in range(columns):
        normed = normalize(x[column], average)
        query[column] = (nt(normed, wq_t) * width ** (-0.5)).astype(bf16)
        keys[column] = nt(normed, wk_t).astype(bf16)
        values_t[column] = nt(wv_t, normed).astype(bf16)
        gate_t[column] = jax.nn.sigmoid(nt(wg_t, normed)).astype(bf16)

    all_b.wait_recv()
    head_of_lane = iota((total, heads * width), 1) // width

    def attend(place):
        span = lanes_at(place)
        penalty = jnp.where(chain_column[...] == chain_row[:1, span], 0.0, -chain_penalty)
        for head in range(heads):
            added = bias[head, :, span].astype(f32) + penalty
            share_t = slice(head * width, (head + 1) * width)

            def attend_column(column):
                own = keys[column]
                own = jnp.where(head_of_lane == head, own, jnp.zeros_like(own))
                scores = nt(own, query[column, span, :]) + added
                scores = jnp.where(keep[...] > 0.5, scores, masked_score)
                expo = jnp.exp(scores - jnp.max(scores, axis=0, keepdims=True))
                scale = 1.0 / jnp.sum(expo, axis=0, keepdims=True)
                attended = nn(values_t[column, share_t, :], (expo * scale).astype(bf16))
                gated[column, share_t, span] = (
                    gate_t[column, share_t, span].astype(f32) * attended.astype(bf16).astype(f32)
                ).astype(bf16)

            each(columns, attend_column, most=columns if total == LANES else 1)

    each(total // LANES, attend, most=1)

    packed_lanes = columns * width

    def project(place):
        span = lanes_at(place)
        mine = jnp.concatenate([gated[column, :, span] for column in range(columns)], axis=1)
        mine = nt(leave[...], mine).astype(bf16)
        mine = jnp.concatenate(
            [mine[part * LANES : (part + 1) * LANES] for part in range(columns)], axis=1
        )
        update = nn(mine, wide[...]).astype(bf16)
        for part in range(LANES // rows):
            for head in range(heads):
                result[(place * (LANES // rows) + part) * heads + head] = update[
                    part * rows : (part + 1) * rows,
                    head * packed_lanes : (head + 1) * packed_lanes,
                ]

    each(total // LANES, project, most=1)

    def give(pd, ph):
        send(result.at[pd * heads + ph], landed.at[me], r_sem, pd, ph).start()

    others(give)
    landed[me] = result[me]
    for copies in (all_x, all_w, all_wb, all_b):
        copies.wait_send()
    all_r.wait_recv()
    sources = LANES // columns

    def settle(place):
        came = landed[pl.ds(place * sources, sources)].reshape(sources * rows, packed_lanes)
        moved = tn(came, arrive[...]).astype(bf16)
        for row in range(rows):
            part, line = row // columns, row % columns
            out[row, :, lanes_at(place)] = moved[
                line * width : (line + 1) * width, part * LANES : (part + 1) * LANES
            ]

    each(total // LANES, settle, most=1)
    all_r.wait_send()


def body(groups, heads, pair, residue_mask, chain_breaks, w_query, w_key, w_value, w_gate, w_bias, w_out):
    rows, total, channels = pair.shape
    width = w_query.shape[1]
    devices = groups * heads
    columns = total // devices
    packed_lanes = columns * width
    assert packed_lanes == LANES and columns * columns == rows
    dma = pltpu.SemaphoreType.DMA
    update = pl.pallas_call(
        functools.partial(kernel, groups, heads),
        out_shape=jax.ShapeDtypeStruct((rows, width, total), bf16),
        in_specs=[pl.BlockSpec(memory_space=pltpu.HBM)] * 9,
        out_specs=pl.BlockSpec(memory_space=pltpu.VMEM),
        scratch_shapes=[
            pltpu.VMEM((rows, total, channels), bf16),
            pltpu.VMEM((1, total), jnp.int32),
            pltpu.VMEM((1, total), jnp.int32),
            pltpu.VMEM((1, channels), bf16),
            pltpu.VMEM((groups, columns, rows, channels), bf16),
            pltpu.VMEM((columns, total, channels), bf16),
            pltpu.VMEM((heads, 5 * width, channels), bf16),
            pltpu.VMEM((heads, rows, channels), bf16),
            pltpu.VMEM((heads, total, total), bf16),
            pltpu.VMEM((columns * channels, heads * packed_lanes), bf16),
            pltpu.VMEM((total, LANES), f32),
            pltpu.VMEM((8, total), f32),
            pltpu.VMEM((total, LANES), f32),
            pltpu.VMEM((columns, total, channels), bf16),
            pltpu.VMEM((columns, total, channels), bf16),
            pltpu.VMEM((columns, channels, total), bf16),
            pltpu.VMEM((columns, channels, total), bf16),
            pltpu.VMEM((columns, channels, total), bf16),
            pltpu.VMEM((devices, rows, packed_lanes), bf16),
            pltpu.VMEM((devices, rows, packed_lanes), bf16),
            pltpu.VMEM((columns * LANES, columns * LANES), bf16),
            pltpu.VMEM((columns * LANES, columns * LANES), bf16),
            dma((9,)), dma((2,)), dma((2,)), dma((2,)), dma((2,)), dma((2,)),
        ],
        compiler_params=pltpu.CompilerParams(
            collective_id=0, has_side_effects=True, vmem_limit_bytes=58 * 2**20
        ),
    )(
        pair, residue_mask.reshape(1, total), chain_breaks.reshape(1, total),
        w_query.T, w_key.T, w_value.T, w_gate.T, w_bias.T, w_out,
    )
    return jnp.swapaxes(update, 1, 2)


def solution(mesh):
    placed = (
        P("dap", None, None),
        P(),
        P(),
        P(None, "head"),
        P(None, "head"),
        P(None, "head"),
        P(None, "head"),
        P(None, "head"),
        P("head", None),
    )
    return jax.shard_map(
        functools.partial(body, mesh.shape["dap"], mesh.shape["head"]),
        mesh=mesh, in_specs=placed, out_specs=P("dap", None, "head"), check_vma=False,
    )
```

```python
import functools

import jax
import jax.numpy as jnp
from jax import lax
from jax.experimental import pallas as pl
from jax.experimental.pallas import tpu as pltpu
from jax.sharding import PartitionSpec as P

chain_penalty = 2.0
masked_score = -1000000000.0
LANES = 128
MESH = pl.DeviceIdType.MESH
f32 = jnp.float32
bf16 = jnp.bfloat16


def nn(a, b):
    return lax.dot_general(a, b, (((1,), (0,)), ((), ())), preferred_element_type=f32)


def nt(a, b):
    return lax.dot_general(a, b, (((1,), (1,)), ((), ())), preferred_element_type=f32)


def tn(a, b):
    return lax.dot_general(a, b, (((0,), (0,)), ((), ())), preferred_element_type=f32)


def each(count, do, start=0, most=8):
    if count - start <= most:
        for index in range(start, count):
            do(index)
    else:
        pl.loop(start, count)(do)


def lanes_at(place):
    return pl.ds(pl.multiple_of(place * LANES, LANES), LANES)


def ones_where(condition):
    return jnp.where(condition, 1.0, 0.0).astype(bf16)


def iota(shape, axis):
    return lax.broadcasted_iota(jnp.int32, shape, axis)


def normalize(x, average):
    mean = nn(x, average)
    centered = x.astype(f32) - mean
    square = centered * centered
    high = square.astype(bf16)
    low = (square - high.astype(f32)).astype(bf16)
    variance = nn(high, average) + nn(low, average)
    return (centered * lax.rsqrt(variance + 1e-05)).astype(bf16)


def kernel(
    groups, heads,
    pair_in, mask_in, breaks_in, wq, wk, wv, wg, wb_in, wo,
    out,
    pair, mask, breaks, wb, stage, x, weights, wb_all, bias, wide, chain_column, chain_row, keep,
    query, keys, values_t, gate_t, gated, result, landed, leave, arrive,
    in_sem, x_sem, w_sem, wb_sem, b_sem, r_sem,
):
    rows, total, channels = pair.shape
    width = wq.shape[0]
    devices = groups * heads
    block = total // groups
    columns = total // devices
    d = lax.axis_index("dap")
    h = lax.axis_index("head")
    me = d * heads + h
    my_rows = pl.ds(pl.multiple_of(d * rows, rows), rows)

    def around(place, offset, count):
        moved = place + offset
        return jnp.where(moved >= count, moved - count, moved)

    def far(step):
        return around(d, lax.rem(step + groups // 2 - 2, groups - 1) + 1, groups)

    loads = [
        pltpu.make_async_copy(source, target, in_sem.at[place])
        for place, (source, target) in enumerate(
            [(pair_in, pair), (wb_in, wb)]
            + [
                (matrix, weights.at[h, place * width : (place + 1) * width, :])
                for place, matrix in enumerate((wq, wk, wv, wg, wo))
            ]
            + [(mask_in, mask), (breaks_in, breaks)]
        )
    ]
    loads[0].start()

    barrier = pltpu.get_barrier_semaphore()

    def greet(pd, ph):
        pl.semaphore_signal(barrier, inc=1, device_id=(pd, ph), device_id_type=MESH)

    each(groups, lambda step: greet(far(step), h), start=1)
    each(heads, lambda offset: greet(d, around(h, offset, heads)), start=1)
    for load in loads[1:]:
        load.start()

    taken = columns * rows
    in_row = iota((1, rows * block), 1)
    column = lax.rem(in_row, block) - h * columns
    wanted = jnp.where((column >= 0) & (column < columns), column * rows + in_row // block, -1)
    select = ones_where(iota((taken, rows * block), 0) == wanted)

    def selected(group):
        part = pair[:, pl.ds(pl.multiple_of(group * block, block), block), :]
        part = nn(select, part.reshape(rows * block, channels)).astype(bf16)
        return part.reshape(columns, rows, channels)

    loads[1].wait()
    wb_all[h] = jnp.broadcast_to(wb[...].astype(f32), (rows, channels)).astype(bf16)
    pl.semaphore_wait(barrier, groups + heads - 2)

    def send(source, target, sems, pd, ph):
        return pltpu.make_async_remote_copy(
            src_ref=source,
            dst_ref=target,
            send_sem=sems.at[0],
            recv_sem=sems.at[1],
            device_id=(pd, ph),
            device_id_type=MESH,
        )

    def all_copies(part, sems):
        return send(part, part, sems, d, around(h, 1, heads))

    all_x = all_copies(stage.at[pl.ds(0, groups - 1)], x_sem)
    all_w = all_copies(weights.at[pl.ds(0, heads - 1)], w_sem)
    all_wb = all_copies(wb_all.at[pl.ds(0, heads - 1)], wb_sem)
    all_b = all_copies(bias.at[:, pl.ds(0, (groups - 1) * rows), :], b_sem)
    all_r = all_copies(landed.at[pl.ds(0, devices - 1)], r_sem)

    for offset in range(1, heads):
        send(wb_all.at[h], wb_all.at[h], wb_sem, d, around(h, offset, heads)).start()

    loads[0].wait()

    def scatter(step):
        group = far(step)
        stage[step] = selected(group)
        send(stage.at[step], x.at[:, my_rows, :], x_sem, group, h).start()

    each(groups, scatter, start=1)
    x[:, my_rows, :] = selected(d)
    for load in loads[2:]:
        load.wait()
    for offset in range(1, heads):
        send(weights.at[h], weights.at[h], w_sem, d, around(h, offset, heads)).start()

    average = jnp.full((channels, channels), 1.0 / channels, f32).astype(bf16)
    bias_row = lax.rem(iota((heads * rows, LANES), 0), rows)

    def bias_block(place, arrived=True):
        span = lanes_at(place)
        normed = [normalize(pair[row, span, :], average) for row in range(rows)]
        if not arrived:
            all_wb.wait_recv()
        wb_rows = wb_all[...].reshape(heads * rows, channels)
        found = jnp.zeros((heads * rows, LANES), f32)
        for row in range(rows):
            found = jnp.where(bias_row == row, nt(wb_rows, normed[row]), found)
        bias[:, my_rows, span] = found.astype(bf16).reshape(heads, rows, LANES)

    bias_block(0, arrived=False)
    if total > LANES:
        pl.loop(1, total // LANES)(bias_block)

    def share_bias(step):
        part = bias.at[:, my_rows, :]
        send(part, part, b_sem, far(step), h).start()

    each(groups, share_bias, start=1)

    tall = iota((total, total), 0)
    across = iota((total, total), 1)
    breaks_row = jnp.broadcast_to(breaks[...].astype(f32), (LANES, total)).astype(bf16)
    mask_row = jnp.broadcast_to(mask[...].astype(f32), (LANES, total)).astype(bf16)
    chain_column[...] = nt(ones_where(across <= tall), breaks_row)
    keep[...] = nt(ones_where(across == tall), mask_row)
    chain_row[...] = nn(breaks_row[:8], ones_where(tall <= across))

    out_lanes = heads * columns * width
    lane = iota((1, out_lanes), 1)
    lane_column = lax.rem(lane, columns * width) // width
    lane_source = lane // (columns * width) * width + lax.rem(lane, width)
    channel = iota((channels, out_lanes), 0)

    ordered = columns * LANES
    first = iota((ordered, ordered), 0)
    second = iota((1, ordered), 1)
    entry = lax.rem(second, LANES)
    leave[...] = ones_where(
        first
        == lax.rem(entry, columns) * LANES + entry // columns * columns + second // LANES
    )
    arrive[...] = ones_where(
        first
        == entry // columns * rows + second // LANES * columns + lax.rem(entry, columns)
    )

    all_w.wait_recv()
    wo_full = jnp.concatenate([weights[k, 4 * width : 5 * width, :] for k in range(heads)], axis=0)
    for column in range(columns):
        placed = ones_where(channel == jnp.where(lane_column == column, lane_source, -1))
        wide[column * channels : (column + 1) * channels, :] = nn(wo_full, placed).astype(bf16)
    wq_t, wk_t, wv_t, wg_t = (
        jnp.concatenate(
            [weights[k, place * width : (place + 1) * width, :] for k in range(heads)], axis=0
        )
        for place in range(4)
    )

    all_x.wait_recv()
    for column in range(columns):
        normed = normalize(x[column], average)
        query[column] = (nt(normed, wq_t) * width ** (-0.5)).astype(bf16)
        keys[column] = nt(normed, wk_t).astype(bf16)
        values_t[column] = nt(wv_t, normed).astype(bf16)
        gate_t[column] = jax.nn.sigmoid(nt(wg_t, normed)).astype(bf16)

    all_b.wait_recv()
    head_of_lane = iota((total, heads * width), 1) // width

    def attend(place):
        span = lanes_at(place)
        penalty = jnp.where(chain_column[...] == chain_row[:1, span], 0.0, -chain_penalty)
        for head in range(heads):
            added = bias[head, :, span].astype(f32) + penalty
            share_t = slice(head * width, (head + 1) * width)

            def attend_column(column):
                own = keys[column]
                own = jnp.where(head_of_lane == head, own, jnp.zeros_like(own))
                scores = nt(own, query[column, span, :]) + added
                scores = jnp.where(keep[...] > 0.5, scores, masked_score)
                expo = jnp.exp(scores - jnp.max(scores, axis=0, keepdims=True))
                scale = 1.0 / jnp.sum(expo, axis=0, keepdims=True)
                attended = nn(values_t[column, share_t, :], (expo * scale).astype(bf16))
                gated[column, share_t, span] = (
                    gate_t[column, share_t, span].astype(f32) * attended.astype(bf16).astype(f32)
                ).astype(bf16)

            each(columns, attend_column, most=columns if total == LANES else 1)

    each(total // LANES, attend, most=1)

    packed_lanes = columns * width

    def project(place):
        span = lanes_at(place)
        mine = jnp.concatenate([gated[column, :, span] for column in range(columns)], axis=1)
        mine = nt(leave[...], mine).astype(bf16)
        mine = jnp.concatenate(
            [mine[part * LANES : (part + 1) * LANES] for part in range(columns)], axis=1
        )
        update = nn(mine, wide[...]).astype(bf16)
        for part in range(LANES // rows):
            for head in range(heads):
                result[(place * (LANES // rows) + part) * heads + head] = update[
                    part * rows : (part + 1) * rows,
                    head * packed_lanes : (head + 1) * packed_lanes,
                ]

    each(total // LANES, project, most=1)

    def give(pd, ph):
        send(result.at[pd * heads + ph], landed.at[me], r_sem, pd, ph).start()

    for head_offset in range(heads):
        head = around(h, head_offset, heads)
        each(groups, lambda step, head=head: give(far(step), head), start=1)
    each(heads, lambda offset: give(d, around(h, offset, heads)), start=1)
    landed[me] = result[me]
    for copies in (all_x, all_w, all_wb, all_b):
        copies.wait_send()
    all_r.wait_recv()
    sources = LANES // columns

    def settle(place):
        came = landed[pl.ds(place * sources, sources)].reshape(sources * rows, packed_lanes)
        moved = tn(came, arrive[...]).astype(bf16)
        for row in range(rows):
            part, line = row // columns, row % columns
            out[row, :, lanes_at(place)] = moved[
                line * width : (line + 1) * width, part * LANES : (part + 1) * LANES
            ]

    each(total // LANES, settle, most=1)
    all_r.wait_send()


def body(groups, heads, pair, residue_mask, chain_breaks, w_query, w_key, w_value, w_gate, w_bias, w_out):
    rows, total, channels = pair.shape
    width = w_query.shape[1]
    devices = groups * heads
    columns = total // devices
    packed_lanes = columns * width
    assert packed_lanes == LANES and columns * columns == rows
    dma = pltpu.SemaphoreType.DMA
    update = pl.pallas_call(
        functools.partial(kernel, groups, heads),
        out_shape=pltpu.VMEM((rows, width, total), bf16),
        in_specs=[pl.BlockSpec(memory_space=pltpu.HBM)] * 9,
        out_specs=pl.BlockSpec(memory_space=pltpu.VMEM),
        scratch_shapes=[
            pltpu.VMEM((rows, total, channels), bf16),
            pltpu.VMEM((1, total), jnp.int32),
            pltpu.VMEM((1, total), jnp.int32),
            pltpu.VMEM((1, channels), bf16),
            pltpu.VMEM((groups, columns, rows, channels), bf16),
            pltpu.VMEM((columns, total, channels), bf16),
            pltpu.VMEM((heads, 5 * width, channels), bf16),
            pltpu.VMEM((heads, rows, channels), bf16),
            pltpu.VMEM((heads, total, total), bf16),
            pltpu.VMEM((columns * channels, heads * packed_lanes), bf16),
            pltpu.VMEM((total, LANES), f32),
            pltpu.VMEM((8, total), f32),
            pltpu.VMEM((total, LANES), f32),
            pltpu.VMEM((columns, total, channels), bf16),
            pltpu.VMEM((columns, total, channels), bf16),
            pltpu.VMEM((columns, channels, total), bf16),
            pltpu.VMEM((columns, channels, total), bf16),
            pltpu.VMEM((columns, channels, total), bf16),
            pltpu.VMEM((devices, rows, packed_lanes), bf16),
            pltpu.VMEM((devices, rows, packed_lanes), bf16),
            pltpu.VMEM((columns * LANES, columns * LANES), bf16),
            pltpu.VMEM((columns * LANES, columns * LANES), bf16),
            dma((9,)), dma((2,)), dma((2,)), dma((2,)), dma((2,)), dma((2,)),
        ],
        compiler_params=pltpu.CompilerParams(
            collective_id=0, has_side_effects=True, vmem_limit_bytes=52 * 2**20
        ),
    )(
        *(
            pltpu.with_memory_space_constraint(operand, pltpu.HBM)
            for operand in (
                pair, residue_mask.reshape(1, total), chain_breaks.reshape(1, total),
                w_query.T, w_key.T, w_value.T, w_gate.T, w_bias.T, w_out,
            )
        )
    )
    return jnp.swapaxes(update, 1, 2)


def solution(mesh):
    placed = (
        P("dap", None, None),
        P(),
        P(),
        P(None, "head"),
        P(None, "head"),
        P(None, "head"),
        P(None, "head"),
        P(None, "head"),
        P("head", None),
    )
    return jax.shard_map(
        functools.partial(body, mesh.shape["dap"], mesh.shape["head"]),
        mesh=mesh, in_specs=placed, out_specs=P("dap", None, "head"), check_vma=False,
    )
```

```python
import functools

import jax
import jax.numpy as jnp
from jax import lax
from jax.experimental import pallas as pl
from jax.experimental.pallas import tpu as pltpu
from jax.sharding import PartitionSpec as P

chain_penalty = 2.0
masked_score = -1000000000.0
LANES = 128
MESH = pl.DeviceIdType.MESH
f32 = jnp.float32
bf16 = jnp.bfloat16


def nn(a, b):
    return lax.dot_general(a, b, (((1,), (0,)), ((), ())), preferred_element_type=f32)


def nt(a, b):
    return lax.dot_general(a, b, (((1,), (1,)), ((), ())), preferred_element_type=f32)


def tn(a, b):
    return lax.dot_general(a, b, (((0,), (0,)), ((), ())), preferred_element_type=f32)


def each(count, do, start=0, most=8):
    if count - start <= most:
        for index in range(start, count):
            do(index)
    else:
        pl.loop(start, count)(do)


def lanes_at(place):
    return pl.ds(pl.multiple_of(place * LANES, LANES), LANES)


def ones_where(condition):
    return jnp.where(condition, 1.0, 0.0).astype(bf16)


def iota(shape, axis):
    return lax.broadcasted_iota(jnp.int32, shape, axis)


def normalize(x, average):
    mean = nn(x, average)
    centered = x.astype(f32) - mean
    square = centered * centered
    high = square.astype(bf16)
    low = (square - high.astype(f32)).astype(bf16)
    variance = nn(high, average) + nn(low, average)
    return (centered * lax.rsqrt(variance + 1e-05)).astype(bf16)


def kernel(
    groups, heads,
    pair_in, mask_in, breaks_in, wq, wk, wv, wg, wb_in, wo,
    out,
    pair, mask, breaks, wb, stage, x, weights, wb_all, bias, wide, chain_column, chain_row, keep,
    query, keys, values_t, gate_t, gated, result, landed, leave, arrive,
    in_sem, x_sem, w_sem, wb_sem, b_sem, r_sem,
):
    rows, total, channels = pair.shape
    width = wq.shape[0]
    devices = groups * heads
    block = total // groups
    columns = total // devices
    d = lax.axis_index("dap")
    h = lax.axis_index("head")
    me = d * heads + h
    my_rows = pl.ds(pl.multiple_of(d * rows, rows), rows)

    def around(place, offset, count):
        moved = place + offset
        return jnp.where(moved >= count, moved - count, moved)

    def far(step):
        return around(d, lax.rem(step + groups // 2 - 2, groups - 1) + 1, groups)

    loads = [
        pltpu.make_async_copy(source, target, in_sem.at[place])
        for place, (source, target) in enumerate(
            [(pair_in, pair), (wb_in, wb)]
            + [
                (matrix, weights.at[h, place * width : (place + 1) * width, :])
                for place, matrix in enumerate((wq, wk, wv, wg, wo))
            ]
            + [(mask_in, mask), (breaks_in, breaks)]
        )
    ]
    loads[0].start()

    barrier = pltpu.get_barrier_semaphore()

    def greet(pd, ph):
        pl.semaphore_signal(barrier, inc=1, device_id=(pd, ph), device_id_type=MESH)

    each(groups, lambda step: greet(far(step), h), start=1)
    each(heads, lambda offset: greet(d, around(h, offset, heads)), start=1)
    for load in loads[1:]:
        load.start()

    taken = columns * rows
    in_row = iota((1, rows * block), 1)
    column = lax.rem(in_row, block) - h * columns
    wanted = jnp.where((column >= 0) & (column < columns), column * rows + in_row // block, -1)
    select = ones_where(iota((taken, rows * block), 0) == wanted)

    def selected(group):
        part = pair[:, pl.ds(pl.multiple_of(group * block, block), block), :]
        part = nn(select, part.reshape(rows * block, channels)).astype(bf16)
        return part.reshape(columns, rows, channels)

    loads[1].wait()
    wb_all[h] = jnp.broadcast_to(wb[...].astype(f32), (rows, channels)).astype(bf16)
    pl.semaphore_wait(barrier, groups + heads - 2)

    def send(source, target, sems, pd, ph):
        return pltpu.make_async_remote_copy(
            src_ref=source,
            dst_ref=target,
            send_sem=sems.at[0],
            recv_sem=sems.at[1],
            device_id=(pd, ph),
            device_id_type=MESH,
        )

    def all_copies(part, sems):
        return send(part, part, sems, d, around(h, 1, heads))

    all_x = all_copies(stage.at[pl.ds(0, groups - 1)], x_sem)
    all_w = all_copies(weights.at[pl.ds(0, heads - 1)], w_sem)
    all_wb = all_copies(wb_all.at[pl.ds(0, heads - 1)], wb_sem)
    all_b = all_copies(bias.at[:, pl.ds(0, (groups - 1) * rows), :], b_sem)
    all_r = all_copies(landed.at[pl.ds(0, devices - 1)], r_sem)

    for offset in range(1, heads):
        send(wb_all.at[h], wb_all.at[h], wb_sem, d, around(h, offset, heads)).start()

    loads[0].wait()

    def scatter(step):
        group = far(step)
        stage[step] = selected(group)
        send(stage.at[step], x.at[:, my_rows, :], x_sem, group, h).start()

    each(groups, scatter, start=1)
    x[:, my_rows, :] = selected(d)
    for load in loads[2:]:
        load.wait()
    for offset in range(1, heads):
        send(weights.at[h], weights.at[h], w_sem, d, around(h, offset, heads)).start()

    average = jnp.full((channels, channels), 1.0 / channels, f32).astype(bf16)
    bias_row = lax.rem(iota((heads * rows, LANES), 0), rows)

    def bias_block(place, arrived=True):
        span = lanes_at(place)
        normed = [normalize(pair[row, span, :], average) for row in range(rows)]
        if not arrived:
            all_wb.wait_recv()
        wb_rows = wb_all[...].reshape(heads * rows, channels)
        found = jnp.zeros((heads * rows, LANES), f32)
        for row in range(rows):
            found = jnp.where(bias_row == row, nt(wb_rows, normed[row]), found)
        bias[:, my_rows, span] = found.astype(bf16).reshape(heads, rows, LANES)

    bias_block(0, arrived=False)
    if total > LANES:
        pl.loop(1, total // LANES)(bias_block)

    def share_bias(step):
        part = bias.at[:, my_rows, :]
        send(part, part, b_sem, far(step), h).start()

    each(groups, share_bias, start=1)

    tall = iota((total, total), 0)
    across = iota((total, total), 1)
    breaks_row = jnp.broadcast_to(breaks[...].astype(f32), (LANES, total)).astype(bf16)
    mask_row = jnp.broadcast_to(mask[...].astype(f32), (LANES, total)).astype(bf16)
    chain_column[...] = nt(ones_where(across <= tall), breaks_row)
    keep[...] = nt(ones_where(across == tall), mask_row)
    chain_row[...] = nn(breaks_row[:8], ones_where(tall <= across))

    out_lanes = heads * columns * width
    lane = iota((1, out_lanes), 1)
    lane_column = lax.rem(lane, columns * width) // width
    lane_source = lane // (columns * width) * width + lax.rem(lane, width)
    channel = iota((channels, out_lanes), 0)

    ordered = columns * LANES
    first = iota((ordered, ordered), 0)
    second = iota((1, ordered), 1)
    entry = lax.rem(second, LANES)
    leave[...] = ones_where(
        first
        == lax.rem(entry, columns) * LANES + entry // columns * columns + second // LANES
    )
    arrive[...] = ones_where(
        first
        == entry // columns * rows + second // LANES * columns + lax.rem(entry, columns)
    )

    all_w.wait_recv()
    wo_full = jnp.concatenate([weights[k, 4 * width : 5 * width, :] for k in range(heads)], axis=0)
    for column in range(columns):
        placed = ones_where(channel == jnp.where(lane_column == column, lane_source, -1))
        wide[column * channels : (column + 1) * channels, :] = nn(wo_full, placed).astype(bf16)
    wq_t, wk_t, wv_t, wg_t = (
        jnp.concatenate(
            [weights[k, place * width : (place + 1) * width, :] for k in range(heads)], axis=0
        )
        for place in range(4)
    )
    wqk_t = jnp.concatenate([wq_t, wk_t], axis=0)
    wvg_t = jnp.concatenate([wv_t, wg_t], axis=0)
    wide_heads = heads * width

    all_x.wait_recv()
    def project_in(first, count):
        normed = normalize(x[first : first + count].reshape(count * total, channels), average)
        upright = nt(normed, wqk_t)
        turned = nt(wvg_t, normed)
        for column in range(count):
            part = slice(column * total, (column + 1) * total)
            query[first + column] = (upright[part, :wide_heads] * width ** (-0.5)).astype(bf16)
            keys[first + column] = upright[part, wide_heads:].astype(bf16)
            values_t[first + column] = turned[:wide_heads, part].astype(bf16)
            gate_t[first + column] = jax.nn.sigmoid(turned[wide_heads:, part]).astype(bf16)

    together = columns if total == LANES else 1
    for first in range(0, columns, together):
        project_in(first, together)

    all_b.wait_recv()
    head_of_lane = iota((total, wide_heads), 1) // width
    head_of_row = iota((wide_heads, total), 0) // width

    def attend(place):
        span = lanes_at(place)
        penalty = jnp.where(chain_column[...] == chain_row[:1, span], 0.0, -chain_penalty)
        added = [bias[head, :, span].astype(f32) + penalty for head in range(heads)]
        present = keep[...] > 0.5

        def attend_column(column):
            upright, turned = keys[column], values_t[column]
            nothing = jnp.zeros((), bf16)
            own = [jnp.where(head_of_lane == head, upright, nothing) for head in range(heads)]
            scores = nt(jnp.concatenate(own, axis=0), query[column, span, :])
            shares = []
            for head in range(heads):
                mine = scores[head * total : (head + 1) * total] + added[head]
                mine = jnp.where(present, mine, masked_score)
                expo = jnp.exp(mine - jnp.max(mine, axis=0, keepdims=True))
                scale = 1.0 / jnp.sum(expo, axis=0, keepdims=True)
                shares.append((expo * scale).astype(bf16))
            own = [jnp.where(head_of_row == head, turned, nothing) for head in range(heads)]
            attended = nn(jnp.concatenate(own, axis=1), jnp.concatenate(shares, axis=0))
            gated[column, :, span] = (
                gate_t[column, :, span].astype(f32) * attended.astype(bf16).astype(f32)
            ).astype(bf16)

        each(columns, attend_column, most=columns if total == LANES else 1)

    each(total // LANES, attend, most=1)

    packed_lanes = columns * width

    def project(place):
        span = lanes_at(place)
        mine = jnp.concatenate([gated[column, :, span] for column in range(columns)], axis=1)
        mine = nt(leave[...], mine).astype(bf16)
        mine = jnp.concatenate(
            [mine[part * LANES : (part + 1) * LANES] for part in range(columns)], axis=1
        )
        update = nn(mine, wide[...]).astype(bf16)
        for part in range(LANES // rows):
            for head in range(heads):
                result[(place * (LANES // rows) + part) * heads + head] = update[
                    part * rows : (part + 1) * rows,
                    head * packed_lanes : (head + 1) * packed_lanes,
                ]

    each(total // LANES, project, most=1)

    def give(pd, ph):
        send(result.at[pd * heads + ph], landed.at[me], r_sem, pd, ph).start()

    for head_offset in range(heads):
        head = around(h, head_offset, heads)
        each(groups, lambda step, head=head: give(far(step), head), start=1)
    each(heads, lambda offset: give(d, around(h, offset, heads)), start=1)
    landed[me] = result[me]
    for copies in (all_x, all_w, all_wb, all_b):
        copies.wait_send()
    all_r.wait_recv()
    sources = LANES // columns

    def settle(place):
        came = landed[pl.ds(place * sources, sources)].reshape(sources * rows, packed_lanes)
        moved = tn(came, arrive[...]).astype(bf16)
        for row in range(rows):
            part, line = row // columns, row % columns
            out[row, :, lanes_at(place)] = moved[
                line * width : (line + 1) * width, part * LANES : (part + 1) * LANES
            ]

    each(total // LANES, settle, most=1)
    all_r.wait_send()


def body(groups, heads, pair, residue_mask, chain_breaks, w_query, w_key, w_value, w_gate, w_bias, w_out):
    rows, total, channels = pair.shape
    width = w_query.shape[1]
    devices = groups * heads
    columns = total // devices
    packed_lanes = columns * width
    assert packed_lanes == LANES and columns * columns == rows
    dma = pltpu.SemaphoreType.DMA
    update = pl.pallas_call(
        functools.partial(kernel, groups, heads),
        out_shape=pltpu.VMEM((rows, width, total), bf16),
        in_specs=[pl.BlockSpec(memory_space=pltpu.HBM)] * 9,
        out_specs=pl.BlockSpec(memory_space=pltpu.VMEM),
        scratch_shapes=[
            pltpu.VMEM((rows, total, channels), bf16),
            pltpu.VMEM((1, total), jnp.int32),
            pltpu.VMEM((1, total), jnp.int32),
            pltpu.VMEM((1, channels), bf16),
            pltpu.VMEM((groups, columns, rows, channels), bf16),
            pltpu.VMEM((columns, total, channels), bf16),
            pltpu.VMEM((heads, 5 * width, channels), bf16),
            pltpu.VMEM((heads, rows, channels), bf16),
            pltpu.VMEM((heads, total, total), bf16),
            pltpu.VMEM((columns * channels, heads * packed_lanes), bf16),
            pltpu.VMEM((total, LANES), f32),
            pltpu.VMEM((8, total), f32),
            pltpu.VMEM((total, LANES), f32),
            pltpu.VMEM((columns, total, channels), bf16),
            pltpu.VMEM((columns, total, channels), bf16),
            pltpu.VMEM((columns, channels, total), bf16),
            pltpu.VMEM((columns, channels, total), bf16),
            pltpu.VMEM((columns, channels, total), bf16),
            pltpu.VMEM((devices, rows, packed_lanes), bf16),
            pltpu.VMEM((devices, rows, packed_lanes), bf16),
            pltpu.VMEM((columns * LANES, columns * LANES), bf16),
            pltpu.VMEM((columns * LANES, columns * LANES), bf16),
            dma((9,)), dma((2,)), dma((2,)), dma((2,)), dma((2,)), dma((2,)),
        ],
        compiler_params=pltpu.CompilerParams(
            collective_id=0, has_side_effects=True, vmem_limit_bytes=52 * 2**20
        ),
    )(
        *(
            pltpu.with_memory_space_constraint(operand, pltpu.HBM)
            for operand in (
                pair, residue_mask.reshape(1, total), chain_breaks.reshape(1, total),
                w_query.T, w_key.T, w_value.T, w_gate.T, w_bias.T, w_out,
            )
        )
    )
    return jnp.swapaxes(update, 1, 2)


def solution(mesh):
    placed = (
        P("dap", None, None),
        P(),
        P(),
        P(None, "head"),
        P(None, "head"),
        P(None, "head"),
        P(None, "head"),
        P(None, "head"),
        P("head", None),
    )
    return jax.shard_map(
        functools.partial(body, mesh.shape["dap"], mesh.shape["head"]),
        mesh=mesh, in_specs=placed, out_specs=P("dap", None, "head"), check_vma=False,
    )
```

```python
import functools

import jax
import jax.numpy as jnp
from jax import lax
from jax.experimental import pallas as pl
from jax.experimental.pallas import tpu as pltpu
from jax.sharding import PartitionSpec as P

chain_penalty = 2.0
masked_score = -1000000000.0
LANES = 128
MESH = pl.DeviceIdType.MESH
f32 = jnp.float32
bf16 = jnp.bfloat16


def nn(a, b):
    return lax.dot_general(a, b, (((1,), (0,)), ((), ())), preferred_element_type=f32)


def nt(a, b):
    return lax.dot_general(a, b, (((1,), (1,)), ((), ())), preferred_element_type=f32)


def tn(a, b):
    return lax.dot_general(a, b, (((0,), (0,)), ((), ())), preferred_element_type=f32)


def each(count, do, start=0, most=8):
    if count - start <= most:
        for index in range(start, count):
            do(index)
    else:
        pl.loop(start, count)(do)


def lanes_at(place):
    return pl.ds(pl.multiple_of(place * LANES, LANES), LANES)


def ones_where(condition):
    return jnp.where(condition, 1.0, 0.0).astype(bf16)


def iota(shape, axis):
    return lax.broadcasted_iota(jnp.int32, shape, axis)


def normalize(x, average):
    mean = nn(x, average)
    centered = x.astype(f32) - mean
    square = centered * centered
    high = square.astype(bf16)
    low = (square - high.astype(f32)).astype(bf16)
    variance = nn(high, average) + nn(low, average)
    return (centered * lax.rsqrt(variance + 1e-05)).astype(bf16)


def kernel(
    groups, heads,
    pair_in, mask_in, breaks_in, wq, wk, wv, wg, wb_in, wo,
    out,
    pair, mask, breaks, wb, stage, x, weights, wb_all, bias, wide, chain_column, chain_row, keep,
    query, keys, values_t, gate_t, gated, result, landed, leave, arrive,
    pair_sem, in_sem, x_sem, w_sem, wb_sem, b_sem, p_sem, r_sem,
):
    rows, total, channels = pair.shape
    width = wq.shape[0]
    devices = groups * heads
    block = total // groups
    columns = total // devices
    d = lax.axis_index("dap")
    h = lax.axis_index("head")
    me = d * heads + h
    half_heads = heads // 2
    mine_first = lax.rem(h, 2) * half_heads
    partner = h + 1 - 2 * lax.rem(h, 2)
    my_heads = pl.ds(mine_first, half_heads)
    my_rows = pl.ds(pl.multiple_of(d * rows, rows), rows)

    def around(place, offset, count):
        moved = place + offset
        return jnp.where(moved >= count, moved - count, moved)

    def far(step):
        return around(d, lax.rem(step + groups // 2 - 2, groups - 1) + 1, groups)

    loads = [
        pltpu.make_async_copy(source, target, in_sem.at[place])
        for place, (source, target) in enumerate(
            [(wb_in, wb)]
            + [
                (matrix, weights.at[h, place * width : (place + 1) * width, :])
                for place, matrix in enumerate((wq, wk, wv, wg, wo))
            ]
            + [(mask_in, mask), (breaks_in, breaks)]
        )
    ]

    def load_pair(group):
        part = pl.ds(pl.multiple_of(group * block, block), block)
        return pltpu.make_async_copy(pair_in.at[:, part], pair.at[:, part], pair_sem.at[group])

    each(groups, lambda step: load_pair(far(step)).start(), start=1)
    load_pair(d).start()

    barrier = pltpu.get_barrier_semaphore()

    def greet(pd, ph):
        pl.semaphore_signal(barrier, inc=1, device_id=(pd, ph), device_id_type=MESH)

    each(groups, lambda step: greet(far(step), h), start=1)
    each(heads, lambda offset: greet(d, around(h, offset, heads)), start=1)
    for load in loads:
        load.start()

    taken = columns * rows
    in_row = iota((1, rows * block), 1)
    column = lax.rem(in_row, block) - h * columns
    wanted = jnp.where((column >= 0) & (column < columns), column * rows + in_row // block, -1)
    select = ones_where(iota((taken, rows * block), 0) == wanted)

    def selected(group):
        part = pair[:, pl.ds(pl.multiple_of(group * block, block), block), :]
        part = nn(select, part.reshape(rows * block, channels)).astype(bf16)
        return part.reshape(columns, rows, channels)

    loads[0].wait()
    wb_all[h] = jnp.broadcast_to(wb[...].astype(f32), (rows, channels)).astype(bf16)
    pl.semaphore_wait(barrier, groups + heads - 2)

    def send(source, target, sems, pd, ph):
        return pltpu.make_async_remote_copy(
            src_ref=source,
            dst_ref=target,
            send_sem=sems.at[0],
            recv_sem=sems.at[1],
            device_id=(pd, ph),
            device_id_type=MESH,
        )

    def all_copies(part, sems):
        return send(part, part, sems, d, around(h, 1, heads))

    all_x = all_copies(stage.at[pl.ds(0, groups - 1)], x_sem)
    all_w = all_copies(weights.at[pl.ds(0, heads - 1)], w_sem)
    all_wb = all_copies(wb_all.at[pl.ds(0, heads - 1)], wb_sem)
    all_b = all_copies(bias.at[pl.ds(0, half_heads), pl.ds(0, (groups - 1) * rows), :], b_sem)
    pass_on = send(bias.at[my_heads], bias.at[my_heads], p_sem, d, partner)
    all_r = all_copies(landed.at[pl.ds(0, devices - 1)], r_sem)

    for offset in range(1, heads):
        send(wb_all.at[h], wb_all.at[h], wb_sem, d, around(h, offset, heads)).start()

    def scatter(first, count):
        steps = [first + index for index in range(count)]
        for step in steps:
            load_pair(far(step)).wait()
        parts = [selected(far(step)) for step in steps]
        for step, part in zip(steps, parts):
            stage[step] = part
        for step in steps:
            send(stage.at[step], x.at[:, my_rows, :], x_sem, far(step), h).start()

    half = groups // 2
    if groups <= 8:
        scatter(1, half)
        scatter(1 + half, groups - 1 - half)
    else:
        pl.loop(1, groups)(lambda step: scatter(step, 1))
    load_pair(d).wait()
    x[:, my_rows, :] = selected(d)
    for load in loads[1:]:
        load.wait()
    for offset in range(1, heads):
        send(weights.at[h], weights.at[h], w_sem, d, around(h, offset, heads)).start()

    average = jnp.full((channels, channels), 1.0 / channels, f32).astype(bf16)
    wb_shape = (half_heads * rows, rows * channels)
    wb_place = lax.rem(iota(wb_shape, 0), rows) == iota(wb_shape, 1) // channels
    chunk = min(rows, 4)

    def bias_block(place, arrived=True):
        span = lanes_at(place)
        normed = []
        for row in range(0, rows, chunk):
            piece = pair[row : row + chunk, span, :].reshape(chunk * LANES, channels)
            piece = normalize(piece, average)
            normed += [piece[line * LANES : (line + 1) * LANES] for line in range(chunk)]
        if not arrived:
            all_wb.wait_recv()
        wb_rows = jnp.concatenate([wb_all[my_heads].reshape(half_heads * rows, channels)] * rows, axis=1)
        wb_rows = jnp.where(wb_place, wb_rows, jnp.zeros((), bf16))
        found = nt(wb_rows, jnp.concatenate(normed, axis=1))
        bias[my_heads, my_rows, span] = found.astype(bf16).reshape(half_heads, rows, LANES)

    bias_block(0, arrived=False)
    if total > LANES:
        pl.loop(1, total // LANES)(bias_block)

    def share_bias(step):
        part = bias.at[my_heads, my_rows, :]
        send(part, part, b_sem, far(step), h).start()

    each(groups, share_bias, start=1)

    tall = iota((total, total), 0)
    across = iota((total, total), 1)
    breaks_row = jnp.broadcast_to(breaks[...].astype(f32), (LANES, total)).astype(bf16)
    mask_row = jnp.broadcast_to(mask[...].astype(f32), (LANES, total)).astype(bf16)
    chain_column[...] = nt(ones_where(across <= tall), breaks_row)
    keep[...] = nt(ones_where(across == tall), mask_row)
    chain_row[...] = nn(breaks_row[:8], ones_where(tall <= across))

    out_lanes = heads * columns * width
    lane = iota((1, out_lanes), 1)
    lane_column = lax.rem(lane, columns * width) // width
    lane_source = lane // (columns * width) * width + lax.rem(lane, width)
    channel = iota((channels, out_lanes), 0)

    ordered = columns * LANES
    first = iota((ordered, ordered), 0)
    second = iota((1, ordered), 1)
    entry = lax.rem(second, LANES)
    leave[...] = ones_where(
        first
        == lax.rem(entry, columns) * LANES + entry // columns * columns + second // LANES
    )

    all_w.wait_recv()
    wo_full = jnp.concatenate([weights[k, 4 * width : 5 * width, :] for k in range(heads)], axis=0)
    for column in range(columns):
        placed = ones_where(channel == jnp.where(lane_column == column, lane_source, -1))
        wide[column * channels : (column + 1) * channels, :] = nn(wo_full, placed).astype(bf16)
    wq_t, wk_t, wv_t, wg_t = (
        jnp.concatenate(
            [weights[k, place * width : (place + 1) * width, :] for k in range(heads)], axis=0
        )
        for place in range(4)
    )
    wqk_t = jnp.concatenate([wq_t, wk_t], axis=0)
    wvg_t = jnp.concatenate([wv_t, wg_t], axis=0)
    wide_heads = heads * width

    all_x.wait_recv()
    def project_in(first, count):
        normed = normalize(x[first : first + count].reshape(count * total, channels), average)
        upright = nt(normed, wqk_t)
        turned = nt(wvg_t, normed)
        for column in range(count):
            part = slice(column * total, (column + 1) * total)
            query[first + column] = (upright[part, :wide_heads] * width ** (-0.5)).astype(bf16)
            keys[first + column] = upright[part, wide_heads:].astype(bf16)
            values_t[first + column] = turned[:wide_heads, part].astype(bf16)
            gate_t[first + column] = jax.nn.sigmoid(turned[wide_heads:, part]).astype(bf16)

    together = columns if total == LANES else 1
    for start in range(0, columns, together):
        project_in(start, together)

    head_of_lane = iota((total, wide_heads), 1) // width
    head_of_row = iota((wide_heads, total), 0) // width
    nothing = jnp.zeros((), bf16)

    order = [around(mine_first, turn, heads) for turn in range(heads)]

    def score(column, span):
        upright = keys[column]
        own = [jnp.where(head_of_lane == head, upright, nothing) for head in order]
        return nt(jnp.concatenate(own, axis=0), query[column, span, :])

    def share(scores, turn, span):
        penalty = jnp.where(chain_column[...] == chain_row[:1, span], 0.0, -chain_penalty)
        added = bias[order[turn], :, span].astype(f32) + penalty
        mine = scores[turn * total : (turn + 1) * total] + added
        mine = jnp.where(keep[...] > 0.5, mine, masked_score)
        expo = jnp.exp(mine - jnp.max(mine, axis=0, keepdims=True))
        scale = 1.0 / jnp.sum(expo, axis=0, keepdims=True)
        return (expo * scale).astype(bf16)

    def attend(column, shares, span):
        turned = values_t[column]
        own = [jnp.where(head_of_row == head, turned, nothing) for head in order]
        attended = nn(jnp.concatenate(own, axis=1), jnp.concatenate(shares, axis=0))
        gated[column, :, span] = (
            gate_t[column, :, span].astype(f32) * attended.astype(bf16).astype(f32)
        ).astype(bf16)

    if total == LANES:
        span = slice(0, LANES)
        scores = [score(column, span) for column in range(columns)]
        all_b.wait_recv()
        pass_on.start()
        shares = [[share(own, turn, span) for turn in range(half_heads)] for own in scores]
        pass_on.wait_recv()
        for column in range(columns):
            later = [share(scores[column], turn, span) for turn in range(half_heads, heads)]
            attend(column, shares[column] + later, span)
    else:
        all_b.wait_recv()
        pass_on.start()
        pass_on.wait_recv()

        @pl.loop(0, total // LANES)
        def _(place):
            span = lanes_at(place)

            @pl.loop(0, columns)
            def _(column):
                own = score(column, span)
                attend(column, [share(own, turn, span) for turn in range(heads)], span)

    packed_lanes = columns * width

    def project(place):
        span = lanes_at(place)
        mine = jnp.concatenate([gated[column, :, span] for column in range(columns)], axis=1)
        mine = nt(leave[...], mine).astype(bf16)
        mine = jnp.concatenate(
            [mine[part * LANES : (part + 1) * LANES] for part in range(columns)], axis=1
        )
        update = nn(mine, wide[...]).astype(bf16)
        for part in range(LANES // rows):
            for head in range(heads):
                result[(place * (LANES // rows) + part) * heads + head] = update[
                    part * rows : (part + 1) * rows,
                    head * packed_lanes : (head + 1) * packed_lanes,
                ]

    each(total // LANES, project, most=1)

    def give(pd, ph):
        send(result.at[pd * heads + ph], landed.at[me], r_sem, pd, ph).start()

    for head_offset in range(heads):
        head = around(h, head_offset, heads)
        each(groups, lambda step, head=head: give(far(step), head), start=1)
    each(heads, lambda offset: give(d, around(h, offset, heads)), start=1)
    landed[me] = result[me]
    arrive[...] = ones_where(
        first
        == entry // columns * rows + second // LANES * columns + lax.rem(entry, columns)
    )
    for copies in (all_x, all_w, all_wb, all_b, pass_on):
        copies.wait_send()
    all_r.wait_recv()
    sources = LANES // columns

    def settle(place):
        came = landed[pl.ds(place * sources, sources)].reshape(sources * rows, packed_lanes)
        moved = tn(came, arrive[...]).astype(bf16)
        for row in range(rows):
            part, line = row // columns, row % columns
            out[row, :, lanes_at(place)] = moved[
                line * width : (line + 1) * width, part * LANES : (part + 1) * LANES
            ]

    each(total // LANES, settle, most=1)
    all_r.wait_send()


def body(groups, heads, pair, residue_mask, chain_breaks, w_query, w_key, w_value, w_gate, w_bias, w_out):
    rows, total, channels = pair.shape
    width = w_query.shape[1]
    devices = groups * heads
    columns = total // devices
    packed_lanes = columns * width
    assert packed_lanes == LANES and columns * columns == rows
    dma = pltpu.SemaphoreType.DMA
    update = pl.pallas_call(
        functools.partial(kernel, groups, heads),
        out_shape=pltpu.VMEM((rows, width, total), bf16),
        in_specs=[pl.BlockSpec(memory_space=pltpu.HBM)] * 9,
        out_specs=pl.BlockSpec(memory_space=pltpu.VMEM),
        scratch_shapes=[
            pltpu.VMEM((rows, total, channels), bf16),
            pltpu.VMEM((1, total), jnp.int32),
            pltpu.VMEM((1, total), jnp.int32),
            pltpu.VMEM((1, channels), bf16),
            pltpu.VMEM((groups, columns, rows, channels), bf16),
            pltpu.VMEM((columns, total, channels), bf16),
            pltpu.VMEM((heads, 5 * width, channels), bf16),
            pltpu.VMEM((heads, rows, channels), bf16),
            pltpu.VMEM((heads, total, total), bf16),
            pltpu.VMEM((columns * channels, heads * packed_lanes), bf16),
            pltpu.VMEM((total, LANES), f32),
            pltpu.VMEM((8, total), f32),
            pltpu.VMEM((total, LANES), f32),
            pltpu.VMEM((columns, total, channels), bf16),
            pltpu.VMEM((columns, total, channels), bf16),
            pltpu.VMEM((columns, channels, total), bf16),
            pltpu.VMEM((columns, channels, total), bf16),
            pltpu.VMEM((columns, channels, total), bf16),
            pltpu.VMEM((devices, rows, packed_lanes), bf16),
            pltpu.VMEM((devices, rows, packed_lanes), bf16),
            pltpu.VMEM((columns * LANES, columns * LANES), bf16),
            pltpu.VMEM((columns * LANES, columns * LANES), bf16),
            dma((groups,)), dma((8,)), dma((2,)), dma((2,)), dma((2,)), dma((2,)), dma((2,)), dma((2,)),
        ],
        compiler_params=pltpu.CompilerParams(
            collective_id=0, has_side_effects=True, vmem_limit_bytes=52 * 2**20
        ),
    )(
        *(
            pltpu.with_memory_space_constraint(operand, pltpu.HBM)
            for operand in (
                pair, residue_mask.reshape(1, total), chain_breaks.reshape(1, total),
                w_query.T, w_key.T, w_value.T, w_gate.T, w_bias.T, w_out,
            )
        )
    )
    return jnp.swapaxes(update, 1, 2)


def solution(mesh):
    placed = (
        P("dap", None, None),
        P(),
        P(),
        P(None, "head"),
        P(None, "head"),
        P(None, "head"),
        P(None, "head"),
        P(None, "head"),
        P("head", None),
    )
    return jax.shard_map(
        functools.partial(body, mesh.shape["dap"], mesh.shape["head"]),
        mesh=mesh, in_specs=placed, out_specs=P("dap", None, "head"), check_vma=False,
    )
```

```python
import functools

import jax
import jax.numpy as jnp
from jax import lax
from jax.experimental import pallas as pl
from jax.experimental.pallas import tpu as pltpu
from jax.sharding import PartitionSpec as P

chain_penalty = 2.0
masked_score = -1000000000.0
LANES = 128
MESH = pl.DeviceIdType.MESH
f32 = jnp.float32
bf16 = jnp.bfloat16


def nn(a, b):
    return lax.dot_general(a, b, (((1,), (0,)), ((), ())), preferred_element_type=f32)


def nt(a, b):
    return lax.dot_general(a, b, (((1,), (1,)), ((), ())), preferred_element_type=f32)


def tn(a, b):
    return lax.dot_general(a, b, (((0,), (0,)), ((), ())), preferred_element_type=f32)


def each(count, do, start=0, most=8):
    if count - start <= most:
        for index in range(start, count):
            do(index)
    else:
        pl.loop(start, count)(do)


def lanes_at(place):
    return pl.ds(pl.multiple_of(place * LANES, LANES), LANES)


def ones_where(condition):
    return jnp.where(condition, 1.0, 0.0).astype(bf16)


def iota(shape, axis):
    return lax.broadcasted_iota(jnp.int32, shape, axis)


def normalize(x, average):
    mean = nn(x, average)
    centered = x.astype(f32) - mean
    square = centered * centered
    high = square.astype(bf16)
    low = (square - high.astype(f32)).astype(bf16)
    variance = nn(high, average) + nn(low, average)
    return (centered * lax.rsqrt(variance + 1e-05)).astype(bf16)


def kernel(
    groups, heads,
    pair_in, mask_in, breaks_in, wq, wk, wv, wg, wb_in, wo,
    out,
    pair, mask, breaks, wb, stage, x, weights, wb_all, bias, wide, chain_column, chain_row, keep,
    query, keys, values_t, gate_t, gated, result, landed, leave, arrive,
    pair_sem, in_sem, x_sem, w_sem, wb_sem, b_sem, p_sem, r_sem,
):
    rows, total, channels = pair.shape
    width = wq.shape[0]
    devices = groups * heads
    block = total // groups
    columns = total // devices
    d = lax.axis_index("dap")
    h = lax.axis_index("head")
    me = d * heads + h
    half_heads = heads // 2
    mine_first = lax.rem(h, 2) * half_heads
    partner = h + 1 - 2 * lax.rem(h, 2)
    my_heads = pl.ds(mine_first, half_heads)
    halved = total == LANES
    span_block = LANES // 2 if halved else LANES
    half_groups = groups // 2
    my_rows = pl.ds(pl.multiple_of(d * rows, rows), rows)

    def around(place, offset, count):
        moved = place + offset
        return jnp.where(moved >= count, moved - count, moved)

    def far(step):
        return around(d, lax.rem(step + groups // 2 - 2, groups - 1) + 1, groups)

    loads = [
        pltpu.make_async_copy(source, target, in_sem.at[place])
        for place, (source, target) in enumerate(
            [(wb_in, wb)]
            + [
                (matrix, weights.at[h, place * width : (place + 1) * width, :])
                for place, matrix in enumerate((wq, wk, wv, wg, wo))
            ]
            + [(mask_in, mask), (breaks_in, breaks)]
        )
    ]

    def load_pair(group):
        part = pl.ds(pl.multiple_of(group * block, block), block)
        return pltpu.make_async_copy(pair_in.at[:, part], pair.at[:, part], pair_sem.at[group])

    each(groups, lambda step: load_pair(far(step)).start(), start=1)
    load_pair(d).start()

    barrier = pltpu.get_barrier_semaphore()

    def greet(pd, ph):
        pl.semaphore_signal(barrier, inc=1, device_id=(pd, ph), device_id_type=MESH)

    each(groups, lambda step: greet(far(step), h), start=1)
    each(heads, lambda offset: greet(d, around(h, offset, heads)), start=1)
    for load in loads:
        load.start()

    taken = columns * rows
    in_row = iota((1, rows * block), 1)
    column = lax.rem(in_row, block) - h * columns
    wanted = jnp.where((column >= 0) & (column < columns), column * rows + in_row // block, -1)
    select = ones_where(iota((taken, rows * block), 0) == wanted)

    def selected(group):
        part = pair[:, pl.ds(pl.multiple_of(group * block, block), block), :]
        part = nn(select, part.reshape(rows * block, channels)).astype(bf16)
        return part.reshape(columns, rows, channels)

    loads[0].wait()
    wb_all[h] = jnp.broadcast_to(wb[...].astype(f32), (rows, channels)).astype(bf16)
    pl.semaphore_wait(barrier, groups + heads - 2)

    def send(source, target, sems, pd, ph):
        return pltpu.make_async_remote_copy(
            src_ref=source,
            dst_ref=target,
            send_sem=sems.at[0],
            recv_sem=sems.at[1],
            device_id=(pd, ph),
            device_id_type=MESH,
        )

    def all_copies(part, sems):
        return send(part, part, sems, d, around(h, 1, heads))

    all_x = all_copies(stage.at[pl.ds(0, groups - 1)], x_sem)
    all_w = all_copies(weights.at[pl.ds(0, heads - 1)], w_sem)
    all_wb = all_copies(wb_all.at[pl.ds(0, heads - 1)], wb_sem)
    all_b = all_copies(bias.at[pl.ds(0, half_heads), pl.ds(0, (groups - 1) * rows), :], b_sem)
    pass_on = send(bias.at[my_heads], bias.at[my_heads], p_sem, d, partner)
    all_r = all_copies(landed.at[pl.ds(0, devices - 1)], r_sem)

    for offset in range(1, heads):
        send(wb_all.at[h], wb_all.at[h], wb_sem, d, around(h, offset, heads)).start()

    def scatter(first, count):
        steps = [first + index for index in range(count)]
        for step in steps:
            load_pair(far(step)).wait()
        parts = [selected(far(step)) for step in steps]
        for step, part in zip(steps, parts):
            stage[step] = part
        for step in steps:
            send(stage.at[step], x.at[:, my_rows, :], x_sem, far(step), h).start()

    half = groups // 2
    if groups <= 8:
        scatter(1, half)
        scatter(1 + half, groups - 1 - half)
    else:
        pl.loop(1, groups)(lambda step: scatter(step, 1))
    load_pair(d).wait()
    x[:, my_rows, :] = selected(d)
    for load in loads[1:]:
        load.wait()
    for offset in range(1, heads):
        send(weights.at[h], weights.at[h], w_sem, d, around(h, offset, heads)).start()

    average = jnp.full((channels, channels), 1.0 / channels, f32).astype(bf16)
    wb_shape = (half_heads * rows, rows * channels)
    wb_place = lax.rem(iota(wb_shape, 0), rows) == iota(wb_shape, 1) // channels
    chunk = min(rows, 4)

    def bias_block(place, arrived=True):
        span = lanes_at(place)
        normed = []
        for row in range(0, rows, chunk):
            piece = pair[row : row + chunk, span, :].reshape(chunk * LANES, channels)
            piece = normalize(piece, average)
            normed += [piece[line * LANES : (line + 1) * LANES] for line in range(chunk)]
        if not arrived:
            all_wb.wait_recv()
        wb_rows = jnp.concatenate([wb_all[my_heads].reshape(half_heads * rows, channels)] * rows, axis=1)
        wb_rows = jnp.where(wb_place, wb_rows, jnp.zeros((), bf16))
        found = nt(wb_rows, jnp.concatenate(normed, axis=1))
        bias[my_heads, my_rows, span] = found.astype(bf16).reshape(half_heads, rows, LANES)

    bias_block(0, arrived=False)
    if total > LANES:
        pl.loop(1, total // LANES)(bias_block)

    def share_bias(step):
        part = bias.at[my_heads, my_rows, :]
        send(part, part, b_sem, far(step), h).start()

    each(groups, share_bias, start=1)

    tall = iota((total, total), 0)
    across = iota((total, total), 1)
    breaks_row = jnp.broadcast_to(breaks[...].astype(f32), (LANES, total)).astype(bf16)
    mask_row = jnp.broadcast_to(mask[...].astype(f32), (LANES, total)).astype(bf16)
    chain_column[...] = nt(ones_where(across <= tall), breaks_row)
    keep[...] = nt(ones_where(across == tall), mask_row)
    chain_row[...] = nn(breaks_row[:8], ones_where(tall <= across))

    out_lanes = heads * columns * width
    lane = iota((1, out_lanes), 1)
    lane_column = lax.rem(lane, columns * width) // width
    lane_source = lane // (columns * width) * width + lax.rem(lane, width)
    channel = iota((channels, out_lanes), 0)

    ordered = columns * span_block
    first = iota((ordered, ordered), 0)
    second = iota((1, ordered), 1)
    entry = lax.rem(second, span_block)
    leave[...] = ones_where(
        first
        == lax.rem(entry, columns) * span_block
        + entry // columns * columns
        + second // span_block
    )

    all_w.wait_recv()
    wo_full = jnp.concatenate([weights[k, 4 * width : 5 * width, :] for k in range(heads)], axis=0)
    for column in range(columns):
        placed = ones_where(channel == jnp.where(lane_column == column, lane_source, -1))
        wide[column * channels : (column + 1) * channels, :] = nn(wo_full, placed).astype(bf16)
    wq_t, wk_t, wv_t, wg_t = (
        jnp.concatenate(
            [weights[k, place * width : (place + 1) * width, :] for k in range(heads)], axis=0
        )
        for place in range(4)
    )
    wqk_t = jnp.concatenate([wq_t, wk_t], axis=0)
    wide_heads = heads * width

    all_x.wait_recv()
    def project_in(first, count):
        normed = normalize(x[first : first + count].reshape(count * total, channels), average)
        upright = nt(normed, wqk_t)
        turned = nt(wv_t, normed)
        ordered_rows = normed
        if halved:
            ordered_rows = jnp.concatenate(
                [
                    normed[column * total + part * span_block :][:span_block]
                    for part in range(2)
                    for column in range(count)
                ],
                axis=0,
            )
        gates = jax.nn.sigmoid(nt(wg_t, ordered_rows)).astype(bf16)
        for column in range(count):
            part = slice(column * total, (column + 1) * total)
            query[first + column] = (upright[part, :wide_heads] * width ** (-0.5)).astype(bf16)
            keys[first + column] = upright[part, wide_heads:].astype(bf16)
            values_t[first + column] = turned[:, part].astype(bf16)
            gate_t[first + column] = gates[:, part]

    together = columns if total == LANES else 1
    for start in range(0, columns, together):
        project_in(start, together)

    head_of_lane = iota((total, wide_heads), 1) // width
    head_of_row = iota((wide_heads, total), 0) // width
    nothing = jnp.zeros((), bf16)

    order = [around(mine_first, turn, heads) for turn in range(heads)]

    def key_rows(column):
        upright = keys[column]
        own = [jnp.where(head_of_lane == head, upright, nothing) for head in order]
        return jnp.concatenate(own, axis=0)

    def value_rows(column):
        turned = values_t[column]
        own = [jnp.where(head_of_row == head, turned, nothing) for head in order]
        return jnp.concatenate(own, axis=1)

    def share(scores, turn, added, bound):
        mine = jnp.minimum(scores[turn * total : (turn + 1) * total] + added, bound)
        expo = jnp.exp(mine - jnp.max(mine, axis=0, keepdims=True))
        scale = 1.0 / jnp.sum(expo, axis=0, keepdims=True)
        return (expo * scale).astype(bf16)

    def penalty(span):
        return jnp.where(chain_column[...] == chain_row[:1, span], 0.0, -chain_penalty)

    def gate_with(gate, attended):
        return (gate.astype(f32) * attended.astype(bf16).astype(f32)).astype(bf16)

    bound = jnp.where(keep[...] > 0.5, 3e38, masked_score)
    packed_lanes = columns * width

    def project(mine, first_group):
        mine = nt(leave[...], mine).astype(bf16)
        mine = jnp.concatenate(
            [mine[part * span_block : (part + 1) * span_block] for part in range(columns)], axis=1
        )
        update = nn(mine, wide[...]).astype(bf16)
        for part in range(span_block // rows):
            for head in range(heads):
                result[(first_group + part) * heads + head] = update[
                    part * rows : (part + 1) * rows,
                    head * packed_lanes : (head + 1) * packed_lanes,
                ]

    def give(pd, ph):
        send(result.at[pd * heads + ph], landed.at[me], r_sem, pd, ph).start()

    if halved:
        near = d // half_groups
        pairs = range(columns // 2)
        key_pairs = [
            jnp.concatenate([key_rows(2 * pair_of), key_rows(2 * pair_of + 1)], axis=1)
            for pair_of in pairs
        ]
        value_pairs = [
            jnp.concatenate([value_rows(2 * pair_of), value_rows(2 * pair_of + 1)], axis=0)
            for pair_of in pairs
        ]
        left = iota((total, LANES), 1) < span_block
        blank = jnp.zeros((span_block, wide_heads), bf16)

        def score_pair(part, pair_of):
            place = pl.ds(pl.multiple_of(part * span_block, span_block), span_block)
            one = jnp.concatenate([query[2 * pair_of, place, :], blank], axis=1)
            two = jnp.concatenate([blank, query[2 * pair_of + 1, place, :]], axis=1)
            return nt(key_pairs[pair_of], jnp.concatenate([one, two], axis=0))

        parts = (1 - near, near)
        scores = [[score_pair(part, pair_of) for pair_of in pairs] for part in parts]
        chains = penalty(slice(0, LANES))
        kept = [iota((total, LANES), 1) // span_block == part for part in parts]

        def added(turn):
            whole = bias[order[turn]].astype(f32) + chains
            turned = pltpu.roll(whole, span_block, 1)
            return [jnp.where(own, whole, turned) for own in kept]

        def shares_of(which, turn, extra):
            return [share(scores[which][p], turn, extra[which], bound) for p in pairs]

        def finish(which, shares):
            part = parts[which]
            mine = []
            for p in pairs:
                stacked = jnp.concatenate([shares[turn][p] for turn in range(heads)], axis=0)
                both = nn(value_pairs[p], stacked)
                attended = jnp.where(left, both[:wide_heads], both[wide_heads:])
                mine.append(gate_with(gate_t[part * (columns // 2) + p], attended))
            project(jnp.concatenate(mine, axis=1), part * half_groups)

        all_b.wait_recv()
        pass_on.start()
        extras = [added(turn) for turn in range(half_heads)]
        shares = [shares_of(0, turn, extras[turn]) for turn in range(half_heads)]
        pass_on.wait_recv()
        extras += [added(turn) for turn in range(half_heads, heads)]
        shares += [shares_of(0, turn, extras[turn]) for turn in range(half_heads, heads)]
        finish(0, shares)
        in_half = d - near * half_groups
        for head_offset in range(heads):
            for step in range(half_groups):
                group = parts[0] * half_groups + around(in_half, step, half_groups)
                give(group, around(h, head_offset, heads))
        finish(1, [shares_of(1, turn, extras[turn]) for turn in range(heads)])
        for head_offset in range(heads):
            for step in range(1, half_groups):
                group = near * half_groups + around(in_half, step, half_groups)
                give(group, around(h, head_offset, heads))
    else:
        all_b.wait_recv()
        pass_on.start()
        pass_on.wait_recv()

        @pl.loop(0, total // LANES)
        def _(place):
            span = lanes_at(place)

            @pl.loop(0, columns)
            def _(column):
                scores = nt(key_rows(column), query[column, span, :])
                stacked = []
                for turn in range(heads):
                    added = bias[order[turn], :, span].astype(f32) + penalty(span)
                    stacked.append(share(scores, turn, added, bound))
                attended = nn(value_rows(column), jnp.concatenate(stacked, axis=0))
                gated[column, :, span] = gate_with(gate_t[column, :, span], attended)

        @pl.loop(0, total // LANES)
        def _(place):
            span = lanes_at(place)
            mine = [gated[column, :, span] for column in range(columns)]
            project(jnp.concatenate(mine, axis=1), place * (LANES // rows))

        for head_offset in range(heads):
            head = around(h, head_offset, heads)
            each(groups, lambda step, head=head: give(far(step), head), start=1)
    each(heads, lambda offset: give(d, around(h, offset, heads)), start=1)
    landed[me] = result[me]
    ordered = columns * LANES
    first = iota((ordered, ordered), 0)
    second = iota((1, ordered), 1)
    entry = lax.rem(second, LANES)
    arrive[...] = ones_where(
        first
        == entry // columns * rows + second // LANES * columns + lax.rem(entry, columns)
    )
    for copies in (all_x, all_w, all_wb, all_b, pass_on):
        copies.wait_send()
    all_r.wait_recv()
    sources = LANES // columns

    def settle(place):
        came = landed[pl.ds(place * sources, sources)].reshape(sources * rows, packed_lanes)
        moved = tn(came, arrive[...]).astype(bf16)
        for row in range(rows):
            part, line = row // columns, row % columns
            out[row, :, lanes_at(place)] = moved[
                line * width : (line + 1) * width, part * LANES : (part + 1) * LANES
            ]

    each(total // LANES, settle, most=1)
    all_r.wait_send()


def body(groups, heads, pair, residue_mask, chain_breaks, w_query, w_key, w_value, w_gate, w_bias, w_out):
    rows, total, channels = pair.shape
    width = w_query.shape[1]
    devices = groups * heads
    columns = total // devices
    packed_lanes = columns * width
    span_block = LANES // 2 if total == LANES else LANES
    assert packed_lanes == LANES and columns * columns == rows
    dma = pltpu.SemaphoreType.DMA
    update = pl.pallas_call(
        functools.partial(kernel, groups, heads),
        out_shape=pltpu.VMEM((rows, width, total), bf16),
        in_specs=[pl.BlockSpec(memory_space=pltpu.HBM)] * 9,
        out_specs=pl.BlockSpec(memory_space=pltpu.VMEM),
        scratch_shapes=[
            pltpu.VMEM((rows, total, channels), bf16),
            pltpu.VMEM((1, total), jnp.int32),
            pltpu.VMEM((1, total), jnp.int32),
            pltpu.VMEM((1, channels), bf16),
            pltpu.VMEM((groups, columns, rows, channels), bf16),
            pltpu.VMEM((columns, total, channels), bf16),
            pltpu.VMEM((heads, 5 * width, channels), bf16),
            pltpu.VMEM((heads, rows, channels), bf16),
            pltpu.VMEM((heads, total, total), bf16),
            pltpu.VMEM((columns * channels, heads * packed_lanes), bf16),
            pltpu.VMEM((total, LANES), f32),
            pltpu.VMEM((8, total), f32),
            pltpu.VMEM((total, LANES), f32),
            pltpu.VMEM((columns, total, channels), bf16),
            pltpu.VMEM((columns, total, channels), bf16),
            pltpu.VMEM((columns, channels, total), bf16),
            pltpu.VMEM((columns, channels, total), bf16),
            pltpu.VMEM((columns, channels, total), bf16),
            pltpu.VMEM((devices, rows, packed_lanes), bf16),
            pltpu.VMEM((devices, rows, packed_lanes), bf16),
            pltpu.VMEM((columns * span_block, columns * span_block), bf16),
            pltpu.VMEM((columns * LANES, columns * LANES), bf16),
            dma((groups,)), dma((8,)), dma((2,)), dma((2,)), dma((2,)), dma((2,)), dma((2,)), dma((2,)),
        ],
        compiler_params=pltpu.CompilerParams(
            collective_id=0, has_side_effects=True, vmem_limit_bytes=52 * 2**20
        ),
    )(
        *(
            pltpu.with_memory_space_constraint(operand, pltpu.HBM)
            for operand in (
                pair, residue_mask.reshape(1, total), chain_breaks.reshape(1, total),
                w_query.T, w_key.T, w_value.T, w_gate.T, w_bias.T, w_out,
            )
        )
    )
    return jnp.swapaxes(update, 1, 2)


def solution(mesh):
    placed = (
        P("dap", None, None),
        P(),
        P(),
        P(None, "head"),
        P(None, "head"),
        P(None, "head"),
        P(None, "head"),
        P(None, "head"),
        P("head", None),
    )
    return jax.shard_map(
        functools.partial(body, mesh.shape["dap"], mesh.shape["head"]),
        mesh=mesh, in_specs=placed, out_specs=P("dap", None, "head"), check_vma=False,
    )
```

```python
import functools

import jax
import jax.numpy as jnp
from jax import lax
from jax.experimental import pallas as pl
from jax.experimental.pallas import tpu as pltpu
from jax.sharding import PartitionSpec as P

chain_penalty = 2.0
masked_score = -1000000000.0
LANES = 128
MESH = pl.DeviceIdType.MESH
f32 = jnp.float32
bf16 = jnp.bfloat16


def nn(a, b):
    return lax.dot_general(a, b, (((1,), (0,)), ((), ())), preferred_element_type=f32)


def nt(a, b):
    return lax.dot_general(a, b, (((1,), (1,)), ((), ())), preferred_element_type=f32)


def tn(a, b):
    return lax.dot_general(a, b, (((0,), (0,)), ((), ())), preferred_element_type=f32)


def each(count, do, start=0, most=8):
    if count - start <= most:
        for index in range(start, count):
            do(index)
    else:
        pl.loop(start, count)(do)


def lanes_at(place):
    return pl.ds(pl.multiple_of(place * LANES, LANES), LANES)


def ones_where(condition):
    return jnp.where(condition, 1.0, 0.0).astype(bf16)


def iota(shape, axis):
    return lax.broadcasted_iota(jnp.int32, shape, axis)


def normalize(x, average):
    mean = nn(x, average)
    centered = x.astype(f32) - mean
    square = centered * centered
    high = square.astype(bf16)
    low = (square - high.astype(f32)).astype(bf16)
    variance = nn(high, average) + nn(low, average)
    return (centered * lax.rsqrt(variance + 1e-05)).astype(bf16)


def kernel(
    groups, heads,
    pair_in, mask_in, breaks_in, wq, wk, wv, wg, wb_in, wo,
    out,
    pair, mask, breaks, wb, stage, x, weights, wb_all, bias, wide, chain_column, chain_row, keep,
    query, keys, values_t, gate_t, gated, result, landed, leave, arrive,
    pair_sem, in_sem, x_sem, w_sem, wb_sem, b_sem, p_sem, f_sem, r_sem,
):
    rows, total, channels = pair.shape
    width = wq.shape[0]
    devices = groups * heads
    block = total // groups
    columns = total // devices
    d = lax.axis_index("dap")
    h = lax.axis_index("head")
    me = d * heads + h
    half_heads = heads // 2
    mine_first = lax.rem(h, 2) * half_heads
    partner = h + 1 - 2 * lax.rem(h, 2)
    my_heads = pl.ds(mine_first, half_heads)
    halved = total == LANES
    span_block = LANES // 2 if halved else LANES
    half_groups = groups // 2
    my_rows = pl.ds(pl.multiple_of(d * rows, rows), rows)

    def around(place, offset, count):
        moved = place + offset
        return jnp.where(moved >= count, moved - count, moved)

    def far(step):
        return around(d, lax.rem(step + groups // 2 - 2, groups - 1) + 1, groups)

    loads = [
        pltpu.make_async_copy(source, target, in_sem.at[place])
        for place, (source, target) in enumerate(
            [(wb_in, wb)]
            + [
                (matrix, weights.at[h, place * width : (place + 1) * width, :])
                for place, matrix in enumerate((wq, wk, wv, wg, wo))
            ]
            + [(mask_in, mask), (breaks_in, breaks)]
        )
    ]

    def load_pair(group):
        part = pl.ds(pl.multiple_of(group * block, block), block)
        return pltpu.make_async_copy(pair_in.at[:, part], pair.at[:, part], pair_sem.at[group])

    each(groups, lambda step: load_pair(far(step)).start(), start=1)
    load_pair(d).start()

    barrier = pltpu.get_barrier_semaphore()

    def greet(pd, ph):
        pl.semaphore_signal(barrier, inc=1, device_id=(pd, ph), device_id_type=MESH)

    each(groups, lambda step: greet(far(step), h), start=1)
    each(heads, lambda offset: greet(d, around(h, offset, heads)), start=1)
    for load in loads:
        load.start()

    taken = columns * rows
    in_row = iota((1, rows * block), 1)
    column = lax.rem(in_row, block) - h * columns
    wanted = jnp.where((column >= 0) & (column < columns), column * rows + in_row // block, -1)
    select = ones_where(iota((taken, rows * block), 0) == wanted)

    def selected(group):
        part = pair[:, pl.ds(pl.multiple_of(group * block, block), block), :]
        part = nn(select, part.reshape(rows * block, channels)).astype(bf16)
        return part.reshape(columns, rows, channels)

    loads[0].wait()
    wb_all[h] = jnp.broadcast_to(wb[...].astype(f32), (rows, channels)).astype(bf16)
    pl.semaphore_wait(barrier, groups + heads - 2)

    def send(source, target, sems, pd, ph):
        return pltpu.make_async_remote_copy(
            src_ref=source,
            dst_ref=target,
            send_sem=sems.at[0],
            recv_sem=sems.at[1],
            device_id=(pd, ph),
            device_id_type=MESH,
        )

    def all_copies(part, sems):
        return send(part, part, sems, d, around(h, 1, heads))

    all_x = all_copies(stage.at[pl.ds(0, groups - 1)], x_sem)
    all_w = all_copies(weights.at[pl.ds(0, heads - 1)], w_sem)
    all_wb = all_copies(wb_all.at[pl.ds(0, heads - 1)], wb_sem)
    all_b = all_copies(bias.at[pl.ds(0, half_heads), pl.ds(0, (groups - 1) * rows), :], b_sem)
    pass_on = send(bias.at[my_heads], bias.at[my_heads], p_sem, d, partner)
    half_devices = devices // 2
    first_r = all_copies(landed.at[pl.ds(0, half_devices)], f_sem)
    all_r = all_copies(landed.at[pl.ds(0, (half_devices if halved else devices) - 1)], r_sem)

    for offset in range(1, heads):
        send(wb_all.at[h], wb_all.at[h], wb_sem, d, around(h, offset, heads)).start()

    def scatter(first, count):
        steps = [first + index for index in range(count)]
        for step in steps:
            load_pair(far(step)).wait()
        parts = [selected(far(step)) for step in steps]
        for step, part in zip(steps, parts):
            stage[step] = part
        for step in steps:
            send(stage.at[step], x.at[:, my_rows, :], x_sem, far(step), h).start()

    half = groups // 2
    if groups <= 8:
        scatter(1, half)
        scatter(1 + half, groups - 1 - half)
    else:
        pl.loop(1, groups)(lambda step: scatter(step, 1))
    load_pair(d).wait()
    x[:, my_rows, :] = selected(d)
    for load in loads[1:]:
        load.wait()
    for offset in range(1, heads):
        send(weights.at[h], weights.at[h], w_sem, d, around(h, offset, heads)).start()

    average = jnp.full((channels, channels), 1.0 / channels, f32).astype(bf16)
    wb_shape = (half_heads * rows, rows * channels)
    wb_place = lax.rem(iota(wb_shape, 0), rows) == iota(wb_shape, 1) // channels
    chunk = min(rows, 4)

    def bias_block(place, arrived=True):
        span = lanes_at(place)
        normed = []
        for row in range(0, rows, chunk):
            piece = pair[row : row + chunk, span, :].reshape(chunk * LANES, channels)
            piece = normalize(piece, average)
            normed += [piece[line * LANES : (line + 1) * LANES] for line in range(chunk)]
        if not arrived:
            all_wb.wait_recv()
        wb_rows = jnp.concatenate([wb_all[my_heads].reshape(half_heads * rows, channels)] * rows, axis=1)
        wb_rows = jnp.where(wb_place, wb_rows, jnp.zeros((), bf16))
        found = nt(wb_rows, jnp.concatenate(normed, axis=1))
        bias[my_heads, my_rows, span] = found.astype(bf16).reshape(half_heads, rows, LANES)

    bias_block(0, arrived=False)
    if total > LANES:
        pl.loop(1, total // LANES)(bias_block)

    def share_bias(step):
        part = bias.at[my_heads, my_rows, :]
        send(part, part, b_sem, far(step), h).start()

    each(groups, share_bias, start=1)

    tall = iota((total, total), 0)
    across = iota((total, total), 1)
    breaks_row = jnp.broadcast_to(breaks[...].astype(f32), (LANES, total)).astype(bf16)
    mask_row = jnp.broadcast_to(mask[...].astype(f32), (LANES, total)).astype(bf16)
    chain_column[...] = nt(ones_where(across <= tall), breaks_row)
    keep[...] = nt(ones_where(across == tall), mask_row)
    chain_row[...] = nn(breaks_row[:8], ones_where(tall <= across))

    out_lanes = heads * columns * width
    lane = iota((1, out_lanes), 1)
    lane_column = lax.rem(lane, columns * width) // width
    lane_source = lane // (columns * width) * width + lax.rem(lane, width)
    channel = iota((channels, out_lanes), 0)

    ordered = columns * span_block
    first = iota((ordered, ordered), 0)
    second = iota((1, ordered), 1)
    entry = lax.rem(second, span_block)
    leave[...] = ones_where(
        first
        == lax.rem(entry, columns) * span_block
        + entry // columns * columns
        + second // span_block
    )

    all_w.wait_recv()
    wo_full = jnp.concatenate([weights[k, 4 * width : 5 * width, :] for k in range(heads)], axis=0)
    for column in range(columns):
        placed = ones_where(channel == jnp.where(lane_column == column, lane_source, -1))
        wide[column * channels : (column + 1) * channels, :] = nn(wo_full, placed).astype(bf16)
    wq_t, wk_t, wv_t, wg_t = (
        jnp.concatenate(
            [weights[k, place * width : (place + 1) * width, :] for k in range(heads)], axis=0
        )
        for place in range(4)
    )
    wqk_t = jnp.concatenate([wq_t, wk_t], axis=0)
    wide_heads = heads * width

    all_x.wait_recv()
    def project_in(first, count):
        normed = normalize(x[first : first + count].reshape(count * total, channels), average)
        upright = nt(normed, wqk_t)
        turned = nt(wv_t, normed)
        ordered_rows = normed
        if halved:
            ordered_rows = jnp.concatenate(
                [
                    normed[column * total + part * span_block :][:span_block]
                    for part in range(2)
                    for column in range(count)
                ],
                axis=0,
            )
        gates = jax.nn.sigmoid(nt(wg_t, ordered_rows)).astype(bf16)
        for column in range(count):
            part = slice(column * total, (column + 1) * total)
            query[first + column] = (upright[part, :wide_heads] * width ** (-0.5)).astype(bf16)
            keys[first + column] = upright[part, wide_heads:].astype(bf16)
            values_t[first + column] = turned[:, part].astype(bf16)
            gate_t[first + column] = gates[:, part]

    together = columns if total == LANES else 1
    for start in range(0, columns, together):
        project_in(start, together)

    head_of_lane = iota((total, wide_heads), 1) // width
    head_of_row = iota((wide_heads, total), 0) // width
    nothing = jnp.zeros((), bf16)

    order = [around(mine_first, turn, heads) for turn in range(heads)]

    def key_rows(column):
        upright = keys[column]
        own = [jnp.where(head_of_lane == head, upright, nothing) for head in order]
        return jnp.concatenate(own, axis=0)

    def value_rows(column):
        turned = values_t[column]
        own = [jnp.where(head_of_row == head, turned, nothing) for head in order]
        return jnp.concatenate(own, axis=1)

    def share(scores, turn, added, bound):
        mine = jnp.minimum(scores[turn * total : (turn + 1) * total] + added, bound)
        expo = jnp.exp(mine - jnp.max(mine, axis=0, keepdims=True))
        scale = 1.0 / jnp.sum(expo, axis=0, keepdims=True)
        return (expo * scale).astype(bf16)

    def penalty(span):
        return jnp.where(chain_column[...] == chain_row[:1, span], 0.0, -chain_penalty)

    def gate_with(gate, attended):
        return (gate.astype(f32) * attended.astype(bf16).astype(f32)).astype(bf16)

    bound = jnp.where(keep[...] > 0.5, 3e38, masked_score)
    packed_lanes = columns * width

    def project(mine, first_group):
        mine = nt(leave[...], mine).astype(bf16)
        mine = jnp.concatenate(
            [mine[part * span_block : (part + 1) * span_block] for part in range(columns)], axis=1
        )
        update = nn(mine, wide[...]).astype(bf16)
        for part in range(span_block // rows):
            for head in range(heads):
                result[(first_group + part) * heads + head] = update[
                    part * rows : (part + 1) * rows,
                    head * packed_lanes : (head + 1) * packed_lanes,
                ]

    def give(pd, ph, sems=r_sem):
        send(result.at[pd * heads + ph], landed.at[me], sems, pd, ph).start()

    if halved:
        near = d // half_groups
        pairs = range(columns // 2)
        key_pairs = [
            jnp.concatenate([key_rows(2 * pair_of), key_rows(2 * pair_of + 1)], axis=1)
            for pair_of in pairs
        ]
        value_pairs = [
            jnp.concatenate([value_rows(2 * pair_of), value_rows(2 * pair_of + 1)], axis=0)
            for pair_of in pairs
        ]
        left = iota((total, LANES), 1) < span_block
        blank = jnp.zeros((span_block, wide_heads), bf16)

        def score_pair(part, pair_of):
            place = pl.ds(pl.multiple_of(part * span_block, span_block), span_block)
            one = jnp.concatenate([query[2 * pair_of, place, :], blank], axis=1)
            two = jnp.concatenate([blank, query[2 * pair_of + 1, place, :]], axis=1)
            return nt(key_pairs[pair_of], jnp.concatenate([one, two], axis=0))

        parts = (1 - near, near)
        scores = [[score_pair(part, pair_of) for pair_of in pairs] for part in parts]
        chains = penalty(slice(0, LANES))
        kept = [iota((total, LANES), 1) // span_block == part for part in parts]

        def added(turn):
            whole = bias[order[turn]].astype(f32) + chains
            turned = pltpu.roll(whole, span_block, 1)
            return [jnp.where(own, whole, turned) for own in kept]

        def shares_of(which, turn, extra):
            return [share(scores[which][p], turn, extra[which], bound) for p in pairs]

        def finish(which, shares):
            part = parts[which]
            mine = []
            for p in pairs:
                stacked = jnp.concatenate([shares[turn][p] for turn in range(heads)], axis=0)
                both = nn(value_pairs[p], stacked)
                attended = jnp.where(left, both[:wide_heads], both[wide_heads:])
                mine.append(gate_with(gate_t[part * (columns // 2) + p], attended))
            project(jnp.concatenate(mine, axis=1), part * half_groups)

        all_b.wait_recv()
        pass_on.start()
        extras = [added(turn) for turn in range(half_heads)]
        shares = [shares_of(0, turn, extras[turn]) for turn in range(half_heads)]
        pass_on.wait_recv()
        extras += [added(turn) for turn in range(half_heads, heads)]
        shares += [shares_of(0, turn, extras[turn]) for turn in range(half_heads, heads)]
        finish(0, shares)
        in_half = d - near * half_groups
        for head_offset in range(heads):
            for step in range(half_groups):
                group = parts[0] * half_groups + around(in_half, step, half_groups)
                give(group, around(h, head_offset, heads), f_sem)
        finish(1, [shares_of(1, turn, extras[turn]) for turn in range(heads)])
        for head_offset in range(heads):
            for step in range(1, half_groups):
                group = near * half_groups + around(in_half, step, half_groups)
                give(group, around(h, head_offset, heads))
    else:
        all_b.wait_recv()
        pass_on.start()
        pass_on.wait_recv()

        @pl.loop(0, total // LANES)
        def _(place):
            span = lanes_at(place)

            @pl.loop(0, columns)
            def _(column):
                scores = nt(key_rows(column), query[column, span, :])
                stacked = []
                for turn in range(heads):
                    added = bias[order[turn], :, span].astype(f32) + penalty(span)
                    stacked.append(share(scores, turn, added, bound))
                attended = nn(value_rows(column), jnp.concatenate(stacked, axis=0))
                gated[column, :, span] = gate_with(gate_t[column, :, span], attended)

        @pl.loop(0, total // LANES)
        def _(place):
            span = lanes_at(place)
            mine = [gated[column, :, span] for column in range(columns)]
            project(jnp.concatenate(mine, axis=1), place * (LANES // rows))

        for head_offset in range(heads):
            head = around(h, head_offset, heads)
            each(groups, lambda step, head=head: give(far(step), head), start=1)
    each(heads, lambda offset: give(d, around(h, offset, heads)), start=1)
    landed[me] = result[me]
    ordered = columns * LANES
    first = iota((ordered, ordered), 0)
    second = iota((1, ordered), 1)
    entry = lax.rem(second, LANES)
    arrive[...] = ones_where(
        first
        == entry // columns * rows + second // LANES * columns + lax.rem(entry, columns)
    )
    for copies in (all_x, all_w, all_wb, all_b, pass_on):
        copies.wait_send()

    def arranged(first_source, sources):
        came = landed[pl.ds(first_source, sources)].reshape(sources * rows, packed_lanes)
        if not halved:
            return tn(came, arrive[...])
        into = pl.multiple_of(first_source * rows, sources * rows)
        return tn(came, arrive[pl.ds(into, sources * rows), :])

    def settle(place, moved):
        moved = moved.astype(bf16)
        for row in range(rows):
            part, line = row // columns, row % columns
            out[row, :, lanes_at(place)] = moved[
                line * width : (line + 1) * width, part * LANES : (part + 1) * LANES
            ]

    if halved:
        first_r.wait_recv()
        moved = arranged((1 - near) * half_devices, half_devices)
        all_r.wait_recv()
        settle(0, moved + arranged(near * half_devices, half_devices))
        first_r.wait_send()
    else:
        all_r.wait_recv()
        sources = LANES // columns
        pl.loop(0, total // LANES)(lambda place: settle(place, arranged(place * sources, sources)))
    all_r.wait_send()


def body(groups, heads, pair, residue_mask, chain_breaks, w_query, w_key, w_value, w_gate, w_bias, w_out):
    rows, total, channels = pair.shape
    width = w_query.shape[1]
    devices = groups * heads
    columns = total // devices
    packed_lanes = columns * width
    span_block = LANES // 2 if total == LANES else LANES
    assert packed_lanes == LANES and columns * columns == rows
    dma = pltpu.SemaphoreType.DMA
    update = pl.pallas_call(
        functools.partial(kernel, groups, heads),
        out_shape=pltpu.VMEM((rows, width, total), bf16),
        in_specs=[pl.BlockSpec(memory_space=pltpu.HBM)] * 9,
        out_specs=pl.BlockSpec(memory_space=pltpu.VMEM),
        scratch_shapes=[
            pltpu.VMEM((rows, total, channels), bf16),
            pltpu.VMEM((1, total), jnp.int32),
            pltpu.VMEM((1, total), jnp.int32),
            pltpu.VMEM((1, channels), bf16),
            pltpu.VMEM((groups, columns, rows, channels), bf16),
            pltpu.VMEM((columns, total, channels), bf16),
            pltpu.VMEM((heads, 5 * width, channels), bf16),
            pltpu.VMEM((heads, rows, channels), bf16),
            pltpu.VMEM((heads, total, total), bf16),
            pltpu.VMEM((columns * channels, heads * packed_lanes), bf16),
            pltpu.VMEM((total, LANES), f32),
            pltpu.VMEM((8, total), f32),
            pltpu.VMEM((total, LANES), f32),
            pltpu.VMEM((columns, total, channels), bf16),
            pltpu.VMEM((columns, total, channels), bf16),
            pltpu.VMEM((columns, channels, total), bf16),
            pltpu.VMEM((columns, channels, total), bf16),
            pltpu.VMEM((columns, channels, total), bf16),
            pltpu.VMEM((devices, rows, packed_lanes), bf16),
            pltpu.VMEM((devices, rows, packed_lanes), bf16),
            pltpu.VMEM((columns * span_block, columns * span_block), bf16),
            pltpu.VMEM((columns * LANES, columns * LANES), bf16),
            dma((groups,)), dma((8,)), dma((2,)), dma((2,)), dma((2,)), dma((2,)), dma((2,)), dma((2,)), dma((2,)),
        ],
        compiler_params=pltpu.CompilerParams(
            collective_id=0, has_side_effects=True, vmem_limit_bytes=52 * 2**20
        ),
    )(
        *(
            pltpu.with_memory_space_constraint(operand, pltpu.HBM)
            for operand in (
                pair, residue_mask.reshape(1, total), chain_breaks.reshape(1, total),
                w_query.T, w_key.T, w_value.T, w_gate.T, w_bias.T, w_out,
            )
        )
    )
    return jnp.swapaxes(update, 1, 2)


def solution(mesh):
    placed = (
        P("dap", None, None),
        P(),
        P(),
        P(None, "head"),
        P(None, "head"),
        P(None, "head"),
        P(None, "head"),
        P(None, "head"),
        P("head", None),
    )
    return jax.shard_map(
        functools.partial(body, mesh.shape["dap"], mesh.shape["head"]),
        mesh=mesh, in_specs=placed, out_specs=P("dap", None, "head"), check_vma=False,
    )
```

```python
import functools

import jax
import jax.numpy as jnp
from jax import lax
from jax.experimental import pallas as pl
from jax.experimental.pallas import tpu as pltpu
from jax.sharding import PartitionSpec as P

chain_penalty = 2.0
masked_score = -1000000000.0
LANES = 128
MESH = pl.DeviceIdType.MESH
f32 = jnp.float32
bf16 = jnp.bfloat16


def nn(a, b):
    return lax.dot_general(a, b, (((1,), (0,)), ((), ())), preferred_element_type=f32)


def nt(a, b):
    return lax.dot_general(a, b, (((1,), (1,)), ((), ())), preferred_element_type=f32)


def tn(a, b):
    return lax.dot_general(a, b, (((0,), (0,)), ((), ())), preferred_element_type=f32)


def each(count, do, start=0, most=8):
    if count - start <= most:
        for index in range(start, count):
            do(index)
    else:
        pl.loop(start, count)(do)


def lanes_at(place):
    return pl.ds(pl.multiple_of(place * LANES, LANES), LANES)


def ones_where(condition):
    return jnp.where(condition, 1.0, 0.0).astype(bf16)


def iota(shape, axis):
    return lax.broadcasted_iota(jnp.int32, shape, axis)


def normalize(x, average):
    mean = nn(x, average)
    centered = x.astype(f32) - mean
    square = centered * centered
    high = square.astype(bf16)
    low = (square - high.astype(f32)).astype(bf16)
    twice = jnp.concatenate([average, average], axis=0)
    variance = nn(jnp.concatenate([high, low], axis=1), twice)
    return (centered * lax.rsqrt(variance + 1e-05)).astype(bf16)


def kernel(
    groups, heads,
    pair_in, mask_in, breaks_in, wq, wk, wv, wg, wb_in, wo,
    out,
    pair, mask, breaks, wb, stage, x, weights, wb_all, bias, wide, chain_column, chain_row, keep,
    query, keys, values_t, gate_t, gated, result, landed, leave, arrive,
    pair_sem, in_sem, x_sem, w_sem, wb_sem, b_sem, p_sem, f_sem, r_sem,
):
    rows, total, channels = pair.shape
    width = wq.shape[0]
    devices = groups * heads
    block = total // groups
    columns = total // devices
    d = lax.axis_index("dap")
    h = lax.axis_index("head")
    me = d * heads + h
    half_heads = heads // 2
    mine_first = lax.rem(h, 2) * half_heads
    partner = h + 1 - 2 * lax.rem(h, 2)
    my_heads = pl.ds(mine_first, half_heads)
    halved = total == LANES
    span_block = LANES // 2 if halved else LANES
    half_groups = groups // 2
    my_rows = pl.ds(pl.multiple_of(d * rows, rows), rows)

    def around(place, offset, count):
        moved = place + offset
        return jnp.where(moved >= count, moved - count, moved)

    def far(step):
        return around(d, lax.rem(step + groups // 2 - 2, groups - 1) + 1, groups)

    loads = [
        pltpu.make_async_copy(source, target, in_sem.at[place])
        for place, (source, target) in enumerate(
            [(wb_in, wb)]
            + [
                (matrix, weights.at[h, place * width : (place + 1) * width, :])
                for place, matrix in enumerate((wq, wk, wv, wg, wo))
            ]
            + [(mask_in, mask), (breaks_in, breaks)]
        )
    ]

    def load_pair(group):
        part = pl.ds(pl.multiple_of(group * block, block), block)
        return pltpu.make_async_copy(pair_in.at[:, part], pair.at[:, part], pair_sem.at[group])

    each(groups, lambda step: load_pair(far(step)).start(), start=1)
    load_pair(d).start()

    barrier = pltpu.get_barrier_semaphore()

    def greet(pd, ph):
        pl.semaphore_signal(barrier, inc=1, device_id=(pd, ph), device_id_type=MESH)

    each(groups, lambda step: greet(far(step), h), start=1)
    each(heads, lambda offset: greet(d, around(h, offset, heads)), start=1)
    for load in loads:
        load.start()

    taken = columns * rows
    in_row = iota((1, rows * block), 1)
    column = lax.rem(in_row, block) - h * columns
    wanted = jnp.where((column >= 0) & (column < columns), column * rows + in_row // block, -1)
    select = ones_where(iota((taken, rows * block), 0) == wanted)

    def selected(group):
        part = pair[:, pl.ds(pl.multiple_of(group * block, block), block), :]
        part = nn(select, part.reshape(rows * block, channels)).astype(bf16)
        return part.reshape(columns, rows, channels)

    pl.semaphore_wait(barrier, groups + heads - 2)

    def send(source, target, sems, pd, ph):
        return pltpu.make_async_remote_copy(
            src_ref=source,
            dst_ref=target,
            send_sem=sems.at[0],
            recv_sem=sems.at[1],
            device_id=(pd, ph),
            device_id_type=MESH,
        )

    def all_copies(part, sems):
        return send(part, part, sems, d, around(h, 1, heads))

    all_x = all_copies(stage.at[pl.ds(0, groups - 1)], x_sem)
    all_w = all_copies(weights.at[pl.ds(0, heads - 1)], w_sem)
    all_wb = all_copies(wb_all.at[pl.ds(0, heads - 1)], wb_sem)
    all_b = all_copies(bias.at[pl.ds(0, half_heads), pl.ds(0, (groups - 1) * rows), :], b_sem)
    pass_on = send(bias.at[my_heads], bias.at[my_heads], p_sem, d, partner)
    half_devices = devices // 2
    first_r = all_copies(landed.at[pl.ds(0, half_devices)], f_sem)
    all_r = all_copies(landed.at[pl.ds(0, (half_devices if halved else devices) - 1)], r_sem)


    def scatter(first, count):
        steps = [first + index for index in range(count)]
        for step in steps:
            load_pair(far(step)).wait()
        parts = [selected(far(step)) for step in steps]
        for step, part in zip(steps, parts):
            stage[step] = part
        for step in steps:
            send(stage.at[step], x.at[:, my_rows, :], x_sem, far(step), h).start()

    half = groups // 2
    if groups <= 8:
        scatter(1, half)
        scatter(1 + half, groups - 1 - half)
    else:
        pl.loop(1, groups)(lambda step: scatter(step, 1))
    loads[0].wait()
    wb_all[h] = jnp.broadcast_to(wb[...].astype(f32), (rows, channels)).astype(bf16)
    for offset in range(1, heads):
        send(wb_all.at[h], wb_all.at[h], wb_sem, d, around(h, offset, heads)).start()
    load_pair(d).wait()
    x[:, my_rows, :] = selected(d)
    for load in loads[1:]:
        load.wait()
    for offset in range(1, heads):
        send(weights.at[h], weights.at[h], w_sem, d, around(h, offset, heads)).start()

    average = jnp.full((channels, channels), 1.0 / channels, f32).astype(bf16)
    wb_shape = (half_heads * rows, rows * channels)
    wb_place = lax.rem(iota(wb_shape, 0), rows) == iota(wb_shape, 1) // channels
    chunk = min(rows, 4)

    def bias_block(place, arrived=True):
        span = lanes_at(place)
        normed = []
        for row in range(0, rows, chunk):
            piece = pair[row : row + chunk, span, :].reshape(chunk * LANES, channels)
            piece = normalize(piece, average)
            normed += [piece[line * LANES : (line + 1) * LANES] for line in range(chunk)]
        if not arrived:
            all_wb.wait_recv()
        wb_rows = jnp.concatenate([wb_all[my_heads].reshape(half_heads * rows, channels)] * rows, axis=1)
        wb_rows = jnp.where(wb_place, wb_rows, jnp.zeros((), bf16))
        found = nt(wb_rows, jnp.concatenate(normed, axis=1))
        bias[my_heads, my_rows, span] = found.astype(bf16).reshape(half_heads, rows, LANES)

    bias_block(0, arrived=False)
    if total > LANES:
        pl.loop(1, total // LANES)(bias_block)

    def share_bias(step):
        part = bias.at[my_heads, my_rows, :]
        send(part, part, b_sem, far(step), h).start()

    each(groups, share_bias, start=1)

    tall = iota((total, total), 0)
    across = iota((total, total), 1)
    breaks_row = jnp.broadcast_to(breaks[...].astype(f32), (LANES, total)).astype(bf16)
    mask_row = jnp.broadcast_to(mask[...].astype(f32), (LANES, total)).astype(bf16)
    chain_column[...] = nt(ones_where(across <= tall), breaks_row)
    keep[...] = nt(ones_where(across == tall), mask_row)
    chain_row[...] = nn(breaks_row[:8], ones_where(tall <= across))

    out_lanes = heads * columns * width
    lane = iota((1, out_lanes), 1)
    lane_column = lax.rem(lane, columns * width) // width
    lane_source = lane // (columns * width) * width + lax.rem(lane, width)
    channel = iota((channels, out_lanes), 0)

    ordered = columns * span_block
    first = iota((ordered, ordered), 0)
    second = iota((1, ordered), 1)
    entry = lax.rem(second, span_block)
    leave[...] = ones_where(
        first
        == lax.rem(entry, columns) * span_block
        + entry // columns * columns
        + second // span_block
    )

    all_w.wait_recv()
    wo_full = jnp.concatenate([weights[k, 4 * width : 5 * width, :] for k in range(heads)], axis=0)
    for column in range(columns):
        placed = ones_where(channel == jnp.where(lane_column == column, lane_source, -1))
        wide[column * channels : (column + 1) * channels, :] = nn(wo_full, placed).astype(bf16)
    wq_t, wk_t, wv_t, wg_t = (
        jnp.concatenate(
            [weights[k, place * width : (place + 1) * width, :] for k in range(heads)], axis=0
        )
        for place in range(4)
    )
    wqk_t = jnp.concatenate([wq_t, wk_t], axis=0)
    wide_heads = heads * width

    all_x.wait_recv()
    def project_in(first, count):
        normed = normalize(x[first : first + count].reshape(count * total, channels), average)
        upright = nt(normed, wqk_t)
        turned = nt(wv_t, normed)
        ordered_rows = normed
        if halved:
            ordered_rows = jnp.concatenate(
                [
                    normed[column * total + part * span_block :][:span_block]
                    for part in range(2)
                    for column in range(count)
                ],
                axis=0,
            )
        gates = jax.nn.sigmoid(nt(wg_t, ordered_rows)).astype(bf16)
        for column in range(count):
            part = slice(column * total, (column + 1) * total)
            query[first + column] = (upright[part, :wide_heads] * width ** (-0.5)).astype(bf16)
            keys[first + column] = upright[part, wide_heads:].astype(bf16)
            values_t[first + column] = turned[:, part].astype(bf16)
            gate_t[first + column] = gates[:, part]

    together = columns if total == LANES else 1
    for start in range(0, columns, together):
        project_in(start, together)

    head_of_lane = iota((total, wide_heads), 1) // width
    head_of_row = iota((wide_heads, total), 0) // width
    nothing = jnp.zeros((), bf16)

    order = [around(mine_first, turn, heads) for turn in range(heads)]

    def key_rows(column):
        upright = keys[column]
        own = [jnp.where(head_of_lane == head, upright, nothing) for head in order]
        return jnp.concatenate(own, axis=0)

    def value_rows(column):
        turned = values_t[column]
        own = [jnp.where(head_of_row == head, turned, nothing) for head in order]
        return jnp.concatenate(own, axis=1)

    def share(scores, turn, added, bound):
        mine = jnp.minimum(scores[turn * total : (turn + 1) * total] + added, bound)
        expo = jnp.exp(mine - jnp.max(mine, axis=0, keepdims=True))
        scale = 1.0 / jnp.sum(expo, axis=0, keepdims=True)
        return (expo * scale).astype(bf16)

    def penalty(span):
        return jnp.where(chain_column[...] == chain_row[:1, span], 0.0, -chain_penalty)

    def gate_with(gate, attended):
        return (gate.astype(f32) * attended.astype(bf16).astype(f32)).astype(bf16)

    bound = jnp.where(keep[...] > 0.5, 3e38, masked_score)
    packed_lanes = columns * width

    def project(mine, first_group):
        mine = nt(leave[...], mine).astype(bf16)
        mine = jnp.concatenate(
            [mine[part * span_block : (part + 1) * span_block] for part in range(columns)], axis=1
        )
        update = nn(mine, wide[...]).astype(bf16)
        for part in range(span_block // rows):
            for head in range(heads):
                result[(first_group + part) * heads + head] = update[
                    part * rows : (part + 1) * rows,
                    head * packed_lanes : (head + 1) * packed_lanes,
                ]

    def give(pd, ph, sems=r_sem):
        send(result.at[pd * heads + ph], landed.at[me], sems, pd, ph).start()

    if halved:
        near = d // half_groups
        pairs = range(columns // 2)
        key_pairs = [
            jnp.concatenate([key_rows(2 * pair_of), key_rows(2 * pair_of + 1)], axis=1)
            for pair_of in pairs
        ]
        value_pairs = [
            jnp.concatenate([value_rows(2 * pair_of), value_rows(2 * pair_of + 1)], axis=0)
            for pair_of in pairs
        ]
        left = iota((total, LANES), 1) < span_block
        blank = jnp.zeros((span_block, wide_heads), bf16)

        def score_pair(part, pair_of):
            place = pl.ds(pl.multiple_of(part * span_block, span_block), span_block)
            one = jnp.concatenate([query[2 * pair_of, place, :], blank], axis=1)
            two = jnp.concatenate([blank, query[2 * pair_of + 1, place, :]], axis=1)
            return nt(key_pairs[pair_of], jnp.concatenate([one, two], axis=0))

        parts = (1 - near, near)
        scores = [[score_pair(part, pair_of) for pair_of in pairs] for part in parts]
        chains = penalty(slice(0, LANES))
        kept = [iota((total, LANES), 1) // span_block == part for part in parts]

        def added(turn):
            whole = bias[order[turn]].astype(f32) + chains
            turned = pltpu.roll(whole, span_block, 1)
            return [jnp.where(own, whole, turned) for own in kept]

        def shares_of(which, turn, extra):
            return [share(scores[which][p], turn, extra[which], bound) for p in pairs]

        def finish(which, shares):
            part = parts[which]
            mine = []
            for p in pairs:
                stacked = jnp.concatenate([shares[turn][p] for turn in range(heads)], axis=0)
                both = nn(value_pairs[p], stacked)
                attended = jnp.where(left, both[:wide_heads], both[wide_heads:])
                mine.append(gate_with(gate_t[part * (columns // 2) + p], attended))
            project(jnp.concatenate(mine, axis=1), part * half_groups)

        all_b.wait_recv()
        pass_on.start()
        extras = [added(turn) for turn in range(half_heads)]
        shares = [shares_of(0, turn, extras[turn]) for turn in range(half_heads)]
        pass_on.wait_recv()
        extras += [added(turn) for turn in range(half_heads, heads)]
        shares += [shares_of(0, turn, extras[turn]) for turn in range(half_heads, heads)]
        finish(0, shares)
        in_half = d - near * half_groups
        for head_offset in range(heads):
            for step in range(half_groups):
                group = parts[0] * half_groups + around(in_half, step, half_groups)
                give(group, around(h, head_offset, heads), f_sem)
        finish(1, [shares_of(1, turn, extras[turn]) for turn in range(heads)])
        for head_offset in range(heads):
            for step in range(1, half_groups):
                group = near * half_groups + around(in_half, step, half_groups)
                give(group, around(h, head_offset, heads))
    else:
        all_b.wait_recv()
        pass_on.start()
        pass_on.wait_recv()

        @pl.loop(0, total // LANES)
        def _(place):
            span = lanes_at(place)

            @pl.loop(0, columns)
            def _(column):
                scores = nt(key_rows(column), query[column, span, :])
                stacked = []
                for turn in range(heads):
                    added = bias[order[turn], :, span].astype(f32) + penalty(span)
                    stacked.append(share(scores, turn, added, bound))
                attended = nn(value_rows(column), jnp.concatenate(stacked, axis=0))
                gated[column, :, span] = gate_with(gate_t[column, :, span], attended)

        @pl.loop(0, total // LANES)
        def _(place):
            span = lanes_at(place)
            mine = [gated[column, :, span] for column in range(columns)]
            project(jnp.concatenate(mine, axis=1), place * (LANES // rows))

        for head_offset in range(heads):
            head = around(h, head_offset, heads)
            each(groups, lambda step, head=head: give(far(step), head), start=1)
    each(heads, lambda offset: give(d, around(h, offset, heads)), start=1)
    landed[me] = result[me]
    ordered = columns * LANES
    first = iota((ordered, ordered), 0)
    second = iota((1, ordered), 1)
    entry = lax.rem(second, LANES)
    arrive[...] = ones_where(
        first
        == entry // columns * rows + second // LANES * columns + lax.rem(entry, columns)
    )
    for copies in (all_x, all_w, all_wb, all_b, pass_on):
        copies.wait_send()

    def arranged(first_source, sources):
        came = landed[pl.ds(first_source, sources)].reshape(sources * rows, packed_lanes)
        if not halved:
            return tn(came, arrive[...])
        into = pl.multiple_of(first_source * rows, sources * rows)
        return tn(came, arrive[pl.ds(into, sources * rows), :])

    def settle(place, moved):
        moved = moved.astype(bf16)
        for row in range(rows):
            part, line = row // columns, row % columns
            out[row, :, lanes_at(place)] = moved[
                line * width : (line + 1) * width, part * LANES : (part + 1) * LANES
            ]

    if halved:
        first_r.wait_recv()
        moved = arranged((1 - near) * half_devices, half_devices)
        all_r.wait_recv()
        settle(0, moved + arranged(near * half_devices, half_devices))
        first_r.wait_send()
    else:
        all_r.wait_recv()
        sources = LANES // columns
        pl.loop(0, total // LANES)(lambda place: settle(place, arranged(place * sources, sources)))
    all_r.wait_send()


def body(groups, heads, pair, residue_mask, chain_breaks, w_query, w_key, w_value, w_gate, w_bias, w_out):
    rows, total, channels = pair.shape
    width = w_query.shape[1]
    devices = groups * heads
    columns = total // devices
    packed_lanes = columns * width
    span_block = LANES // 2 if total == LANES else LANES
    assert packed_lanes == LANES and columns * columns == rows
    dma = pltpu.SemaphoreType.DMA
    update = pl.pallas_call(
        functools.partial(kernel, groups, heads),
        out_shape=pltpu.VMEM((rows, width, total), bf16),
        in_specs=[pl.BlockSpec(memory_space=pltpu.HBM)] * 9,
        out_specs=pl.BlockSpec(memory_space=pltpu.VMEM),
        scratch_shapes=[
            pltpu.VMEM((rows, total, channels), bf16),
            pltpu.VMEM((1, total), jnp.int32),
            pltpu.VMEM((1, total), jnp.int32),
            pltpu.VMEM((1, channels), bf16),
            pltpu.VMEM((groups, columns, rows, channels), bf16),
            pltpu.VMEM((columns, total, channels), bf16),
            pltpu.VMEM((heads, 5 * width, channels), bf16),
            pltpu.VMEM((heads, rows, channels), bf16),
            pltpu.VMEM((heads, total, total), bf16),
            pltpu.VMEM((columns * channels, heads * packed_lanes), bf16),
            pltpu.VMEM((total, LANES), f32),
            pltpu.VMEM((8, total), f32),
            pltpu.VMEM((total, LANES), f32),
            pltpu.VMEM((columns, total, channels), bf16),
            pltpu.VMEM((columns, total, channels), bf16),
            pltpu.VMEM((columns, channels, total), bf16),
            pltpu.VMEM((columns, channels, total), bf16),
            pltpu.VMEM((columns, channels, total), bf16),
            pltpu.VMEM((devices, rows, packed_lanes), bf16),
            pltpu.VMEM((devices, rows, packed_lanes), bf16),
            pltpu.VMEM((columns * span_block, columns * span_block), bf16),
            pltpu.VMEM((columns * LANES, columns * LANES), bf16),
            dma((groups,)), dma((8,)), dma((2,)), dma((2,)), dma((2,)), dma((2,)), dma((2,)), dma((2,)), dma((2,)),
        ],
        compiler_params=pltpu.CompilerParams(
            collective_id=0, has_side_effects=True, vmem_limit_bytes=52 * 2**20
        ),
    )(
        *(
            pltpu.with_memory_space_constraint(operand, pltpu.HBM)
            for operand in (
                pair, residue_mask.reshape(1, total), chain_breaks.reshape(1, total),
                w_query.T, w_key.T, w_value.T, w_gate.T, w_bias.T, w_out,
            )
        )
    )
    return jnp.swapaxes(update, 1, 2)


def solution(mesh):
    placed = (
        P("dap", None, None),
        P(),
        P(),
        P(None, "head"),
        P(None, "head"),
        P(None, "head"),
        P(None, "head"),
        P(None, "head"),
        P("head", None),
    )
    return jax.shard_map(
        functools.partial(body, mesh.shape["dap"], mesh.shape["head"]),
        mesh=mesh, in_specs=placed, out_specs=P("dap", None, "head"), check_vma=False,
    )
```
